32 devices in a mesh: rep: 4 (over y, x), shard: 8 (over z, core).
Axes of the slice: x: 2, y: 2, z: 4, core: 2. Of those that a mesh axis runs over, the one named last changes fastest.
Arguments:
- features: bfloat16 [16384, 1024], P(('rep', 'shard')), may hold values from -6 to 6
- cotangent: bfloat16 [16384, 1024], P(('rep', 'shard')), may hold values from -6 to 6
- cross_weight: bfloat16 [1024, 1024], replicated, may hold values from -0.1875 to 0.1875
- cross_bias: float32 [1024], replicated, may hold values from -3 to 3
- emb_table: float32 [32768, 128], P('shard'), may hold values from -6 to 6
- row_accum: float32 [32768], P('shard'), may hold values from 0.5 to 50
- send_bags: int32 [32, 8, 256], P(('rep', 'shard')), may hold values from 0 to 3583, as said below
- slot_counts: int32 [32, 8], P(('rep', 'shard')), may hold values from 64 to 256, as said below
- recv_rows: int32 [32, 8, 256], P(('rep', 'shard')), may hold values from 0 to 4095, as said below
- touched_rows: int32 [8, 512], P('shard'), may hold values from 0 to 4095, as said below
Outputs:
- weight_grad: float32 [1024, 1024], replicated
- bias_grad: float32 [1024], replicated
- dense_grad: bfloat16 [16384, 128], P(('rep', 'shard'))
- new_table: float32 [32768, 128], P('shard')
- new_accum: float32 [32768], P('shard')
The draws below stay inside these ranges and needn't reach their ends.
Inputs may be any that keep to these rules, and one draw needn't show every extreme that they name: `send_bags`: bag b * 7 + f of a device is feature f of its sample b. The first slot_counts[d, s] slots of a block are live; in each replica group some shard receives 256 live slots from every device of the group. `recv_rows`: every slot, live or not, names a row listed in touched_rows for the owner's shard. `touched_rows`: ascending and distinct.
All inputs are finite; a program needn't handle non-finite values.
Results may differ from the reference program's by a relative error of at most 0.0055.
Values may be sent and summed in bfloat16 or wider, within the bound.
A program may use at most 128 MiB of HBM per device.

```python
import math
import jax
import jax.numpy as jnp
from jax import lax

E = 128
FEATS = 7
D = 1024
TOK_DEV = 512
TOKENS = 16384
SLOTS = 256
ROWS_DEV = 4096
TOUCHED = 512
N_REP = 4
N_SHARD = 8


def plan_slots(key):
    base = jax.random.fold_in(key, 11)
    keys = jax.random.split(base, 5)
    quarter = SLOTS // 4
    picks = jax.vmap(lambda k: jax.random.permutation(k, ROWS_DEV - 2)[:TOUCHED - 2] + 1)(jax.random.split(keys[0], N_SHARD))
    ends = jnp.broadcast_to(jnp.array([0, ROWS_DEV - 1], jnp.int32), (N_SHARD, 2))
    touched = jnp.sort(jnp.concatenate([ends, picks.astype(jnp.int32)], axis=1), axis=1)
    hot = jax.random.randint(keys[1], (N_REP, 1, 1), 0, N_SHARD).astype(jnp.int32)
    counts = jax.random.randint(keys[2], (N_REP, N_SHARD, N_SHARD), quarter, 3 * quarter + 1).astype(jnp.int32)
    dest = jnp.arange(N_SHARD, dtype=jnp.int32)[None, None, :]
    counts = jnp.where(dest == hot, SLOTS, counts).astype(jnp.int32)
    place = jax.random.randint(keys[3], (N_REP, N_SHARD, N_SHARD, SLOTS), 0, TOUCHED).astype(jnp.int32)
    group = jnp.arange(N_REP, dtype=jnp.int32)[:, None, None, None]
    source = jnp.arange(N_SHARD, dtype=jnp.int32)[None, :, None, None]
    slot = jnp.arange(SLOTS, dtype=jnp.int32)[None, None, None, :]
    cover = source * quarter + slot
    place = jnp.where((group == 0) & (slot < quarter), cover, place).astype(jnp.int32)
    dest_full = jnp.broadcast_to(jnp.arange(N_SHARD, dtype=jnp.int32)[None, None, :, None], place.shape)
    rows = touched[dest_full, place]
    bags = jax.random.randint(keys[4], (N_REP, N_SHARD, N_SHARD, SLOTS), 0, TOK_DEV * FEATS).astype(jnp.int32)
    bags = bags.at[0, 0, 0, 0].set(TOK_DEV * FEATS - 1).at[0, 0, 0, 1].set(0)
    devices = N_REP * N_SHARD
    return (bags.reshape(devices, N_SHARD, SLOTS), counts.reshape(devices, N_SHARD), rows.transpose(0, 2, 1, 3).reshape(devices, N_SHARD, SLOTS), touched)


def draw_send_bags(key, part):
    return plan_slots(key)[0]


def draw_slot_counts(key, part):
    return plan_slots(key)[1]


def draw_recv_rows(key, part):
    return plan_slots(key)[2]


def draw_touched_rows(key, part):
    return plan_slots(key)[3]


def levels(own_key, extent, cuts, smallest, top_value):
    gain, own = 1.0, jax.random.fold_in(own_key, 6)
    for position, shards_of in cuts:
        heights = jnp.exp(jax.random.uniform(jax.random.fold_in(own, position), (shards_of,), jnp.float32, smallest / len(cuts), top_value / len(cuts)))
        gain = gain * jnp.repeat(heights, extent[position] // shards_of).reshape([-1 if axis == position else 1 for axis in range(len(extent))])
    return gain


def noise(own_key, extent, width, limit, cuts=(), held_as=jnp.bfloat16):
    result = width * jax.random.normal(own_key, extent, jnp.float32)
    if cuts:
        result = result * levels(own_key, extent, cuts, -0.22, 0.18)
    return jnp.clip(result, -limit, limit).astype(held_as)


def setup_inputs(seed: int = 0) -> dict:
    seeds = jax.random.split(jax.random.key(seed), 11)
    features = noise(seeds[0], (TOKENS, D), 1.0, 6.0, ((0, 32),))
    cotangent = noise(seeds[1], (TOKENS, D), 1.0, 6.0, ((0, 32),))
    cross_weight = noise(seeds[2], (D, D), D ** -0.5, 0.1875)
    cross_bias = noise(seeds[3], (D,), 0.5, 3.0, (), jnp.float32)
    emb_table = noise(seeds[4], (N_SHARD * ROWS_DEV, E), 1.0, 6.0, ((0, 8),), jnp.float32)
    row_accum = jnp.clip(jnp.exp(math.log(50.0) - 4.6051702 * jax.random.uniform(seeds[5], (N_SHARD * ROWS_DEV,), jnp.float32) ** levels(seeds[5], (N_SHARD * ROWS_DEV,), ((0, 8),), -0.2, 0.2)), 0.5, 50.0)
    send_bags = draw_send_bags(jax.random.fold_in(seeds[10], 71), 0)
    slot_counts = draw_slot_counts(jax.random.fold_in(seeds[10], 71), 0)
    recv_rows = draw_recv_rows(jax.random.fold_in(seeds[10], 71), 0)
    touched_rows = draw_touched_rows(jax.random.fold_in(seeds[10], 71), 0)
    return {"features": features, "cotangent": cotangent, "cross_weight": cross_weight, "cross_bias": cross_bias, "emb_table": emb_table, "row_accum": row_accum, "send_bags": send_bags, "slot_counts": slot_counts, "recv_rows": recv_rows, "touched_rows": touched_rows}


learn_rate = 0.5
keep_rate = 0.9

def adagrad_rows(table_rows, accum_rows, grads):
    new_accum = accum_rows + lax.optimization_barrier(jnp.mean(grads * grads, axis=1))
    new_rows = keep_rate * table_rows - learn_rate * grads / jnp.sqrt(new_accum)[:, None]
    return (new_rows, new_accum)

def reference(features, cotangent, cross_weight, cross_bias, emb_table, row_accum, send_bags, slot_counts, recv_rows, touched_rows):
    scale = 1.0 / jnp.sqrt(jnp.float32(TOKENS))
    linear = jnp.dot(features, cross_weight, preferred_element_type=jnp.float32) + cross_bias
    cot_f = cotangent.astype(jnp.float32)
    gated = (cot_f * features.astype(jnp.float32)).astype(jnp.bfloat16)
    weight_grad = jnp.dot(features.T, gated, preferred_element_type=jnp.float32) * scale
    bias_grad = lax.optimization_barrier(jnp.sum(gated.astype(jnp.float32), axis=0)) * scale
    backprop = jnp.dot(gated, cross_weight.T, preferred_element_type=jnp.float32)
    input_grad = cot_f * linear + backprop + cot_f
    dense_grad = input_grad[:, :E].astype(jnp.bfloat16)
    pooled = input_grad[:, E:].astype(jnp.bfloat16).reshape(TOKENS * FEATS, E)
    devices = N_REP * N_SHARD
    offsets = (jnp.arange(devices, dtype=jnp.int32) * (TOK_DEV * FEATS))[:, None, None]
    slot_grad = pooled[(send_bags + offsets).reshape(-1)].reshape(devices, N_SHARD, SLOTS, E)
    live_mask = jnp.arange(SLOTS, dtype=jnp.int32)[None, None, :] < slot_counts[:, :, None]
    slot_grad = jnp.where(live_mask[..., None], slot_grad, jnp.zeros((), jnp.bfloat16))
    arranged = slot_grad.reshape(N_REP, N_SHARD, N_SHARD, SLOTS, E).transpose(0, 2, 1, 3, 4)
    owners = jnp.arange(N_SHARD, dtype=jnp.int32)[None, :, None, None] * ROWS_DEV
    seg_ids = (recv_rows.reshape(N_REP, N_SHARD, N_SHARD, SLOTS) + owners).reshape(-1)
    row_grad = jax.ops.segment_sum(arranged.reshape(-1, E).astype(jnp.float32), seg_ids, num_segments=N_SHARD * ROWS_DEV)
    listed = (touched_rows + jnp.arange(N_SHARD, dtype=jnp.int32)[:, None] * ROWS_DEV).reshape(-1)
    marks = jnp.zeros((N_SHARD * ROWS_DEV,), jnp.int32).at[listed].set(1) > 0
    upd_table, upd_accum = adagrad_rows(emb_table, row_accum, row_grad)
    new_table = jnp.where(marks[:, None], upd_table, emb_table)
    new_accum = jnp.where(marks, upd_accum, row_accum)
    return (weight_grad, bias_grad, dense_grad, new_table, new_accum)
```

```python
import functools

import jax
import jax.numpy as jnp
from jax import lax
from jax.experimental import pallas as pl
from jax.experimental.pallas import tpu as pltpu
from jax.sharding import PartitionSpec as P

learn_rate = 0.5
keep_rate = 0.9
MESH = pl.DeviceIdType.MESH
F32 = jnp.float32
BF16 = jnp.bfloat16


def step_kernel(
    n_rep,
    n_shard,
    feat_ref,
    cot_ref,
    w_ref,
    cbias_ref,
    code_ref,
    rows_ref,
    touched_ref,
    wsum_ref,
    bsum_ref,
    dense_ref,
    rowt_ref,
    gated,
    ig,
    wown,
    wsend,
    wpair,
    p1buf,
    p2buf,
    p3buf,
    bbuf1,
    bbuf2,
    bbuf3,
    outgoing,
    incoming,
    rowacc,
    rowsend,
    rowbuf,
    p1_sem,
    p2_sem,
    p3_sem,
    b1_sem,
    b2_sem,
    b3_sem,
    a2a_sem,
    rrs_sem,
    rag_sem,
    agz_sem,
    agr_sem,
    agc_sem,
):
    nz = n_shard // 2
    rep = lax.axis_index("rep")
    shard = lax.axis_index("shard")
    core = lax.rem(shard, 2)
    zi = shard // 2
    partner = zi * 2 + (1 - core)
    tok, d = feat_ref.shape
    width = dense_ref.shape[1]
    feats = d // width - 1
    half = d // 2
    rblk = d // n_rep
    zblk = rblk // nz
    touched_count = rowt_ref.shape[0]
    tblk = touched_count // n_rep
    slots = code_ref.shape[1]

    def rep_peer(o):
        return lax.rem(rep + o, n_rep)

    def rep_from(o):
        return lax.rem(rep + n_rep - o, n_rep)

    def z_peer(o):
        return lax.rem(zi + o, nz)

    def z_from(o):
        return lax.rem(zi + nz - o, nz)

    def shard_peer(o):
        return lax.rem(shard + o, n_shard)

    def shard_from(o):
        return lax.rem(shard + n_shard - o, n_shard)

    def remote(src, dst, sems, index, target):
        return pltpu.make_async_remote_copy(
            src_ref=src,
            dst_ref=dst,
            send_sem=sems.at[0, index],
            recv_sem=sems.at[1, index],
            device_id=target,
            device_id_type=MESH,
        )

    barrier = pltpu.get_barrier_semaphore()
    for o in range(1, n_shard):
        pl.semaphore_signal(
            barrier, inc=1, device_id={"shard": shard_peer(o)}, device_id_type=MESH
        )
    for o in range(1, n_rep):
        pl.semaphore_signal(barrier, inc=1, device_id={"rep": rep_peer(o)}, device_id_type=MESH)

    @pl.loop(0, tok // 128)
    def _(i):
        r = pl.ds(pl.multiple_of(i * 128, 128), 128)
        gated[r, :] = (cot_ref[r, :].astype(F32) * feat_ref[r, :].astype(F32)).astype(BF16)

    def weight_half(col_half, out, out_type):
        cols = pl.ds(pl.multiple_of(col_half * half, half), half)

        @pl.loop(0, d // 256)
        def _(i):
            r = pl.ds(pl.multiple_of(i * 256, 256), 256)
            out[r, :] = lax.dot_general(
                feat_ref[:, r], gated[:, cols], (((0,), (0,)), ((), ())), preferred_element_type=F32
            ).astype(out_type)

    weight_half(1 - core, wsend, BF16)
    pl.semaphore_wait(barrier, n_shard - 1 + n_rep - 1)
    p1 = remote(wsend, p1buf, p1_sem, 0, {"shard": partner})
    p1.start()
    weight_half(core, wown, F32)
    bias_row = jnp.sum(gated[...].astype(F32), axis=0, keepdims=True)
    for j in range(d // 128):
        bbuf1[0, pl.ds(j, 1), :] = bias_row[:, j * 128 : (j + 1) * 128]
    b1 = remote(bbuf1.at[0], bbuf1.at[1], b1_sem, 0, {"shard": partner})
    b1.start()

    p1.wait_recv()

    @pl.loop(0, n_rep)
    def _(i):
        r = pl.ds(pl.multiple_of(i * rblk, rblk), rblk)
        wpair[r, :] = (wown[r, :] + p1buf[r, :].astype(F32)).astype(BF16)

    def p2(o):
        target = rep_peer(o)
        r = pl.ds(pl.multiple_of(target * rblk, rblk), rblk)
        return remote(wpair.at[r, :], p2buf.at[o], p2_sem, o, {"rep": target})

    for o in range(1, n_rep):
        p2(o).start()
    b1.wait_recv()
    bbuf2[rep] = bbuf1[0] + bbuf1[1]

    def b2(o, slot):
        return remote(bbuf2.at[slot], bbuf2.at[slot], b2_sem, o, {"rep": rep_peer(o)})

    for o in range(1, n_rep):
        b2(o, rep).start()

    @pl.loop(0, d // 256)
    def _(i):
        c = pl.ds(pl.multiple_of(i * 256, 256), 256)
        linear = jnp.dot(feat_ref[...], w_ref[:, c], preferred_element_type=F32) + cbias_ref[:, c]
        back = lax.dot_general(
            gated[...], w_ref[c, :], (((1,), (1,)), ((), ())), preferred_element_type=F32
        )
        cot = cot_ref[:, c].astype(F32)
        ig[:, c] = (cot * linear + back + cot).astype(BF16)

    dense_ref[...] = ig[:, :width]

    def gather(dest):
        code = jnp.transpose(jnp.broadcast_to(code_ref[pl.ds(dest, 1), :], (128, slots)))
        sample = jnp.right_shift(code, 3)
        feature = jnp.bitwise_and(code, 7)
        lane = lax.broadcasted_iota(jnp.int32, (slots, 128), 1)
        select = jnp.concatenate(
            [jnp.where(sample == lane + k * 128, 1.0, 0.0) for k in range(tok // 128)], axis=1
        ).astype(BF16)
        wide = jnp.dot(select, ig[:, width:], preferred_element_type=F32)
        picked = jnp.zeros((slots, width), F32)
        for f in range(feats):
            picked = jnp.where(feature == f, wide[:, f * width : (f + 1) * width], picked)
        return picked.astype(BF16)

    def a2a(o):
        dest = shard_peer(o)
        return remote(outgoing.at[dest], incoming.at[shard], a2a_sem, o, {"shard": dest})

    def a2a_in(o):
        src = shard_from(o)
        return remote(outgoing.at[src], incoming.at[src], a2a_sem, o, {"shard": src})

    @pl.loop(1, n_shard)
    def _(o):
        outgoing[shard_peer(o)] = gather(shard_peer(o))
        a2a(o).start()

    incoming[shard] = gather(shard)

    for o in range(1, n_rep):
        p2(o).wait_recv()
    own_rows = pl.ds(pl.multiple_of(rep * rblk, rblk), rblk)
    total = wpair[own_rows, :].astype(F32)
    for o in range(1, n_rep):
        total = total + p2buf[o].astype(F32)
    p2buf[0] = total.astype(BF16)

    def p3(o):
        target = z_peer(o)
        r = pl.ds(pl.multiple_of(target * zblk, zblk), zblk)
        return remote(p2buf.at[0, r, :], p3buf.at[o], p3_sem, o, {"shard": target * 2 + core})

    for o in range(1, nz):
        p3(o).start()
    for o in range(1, n_rep):
        b2(o, rep_from(o)).wait_recv()
    bias_rep = bbuf2[0]
    for q in range(1, n_rep):
        bias_rep = bias_rep + bbuf2[q]
    bbuf3[zi] = bias_rep

    def b3(o, slot):
        return remote(
            bbuf3.at[slot], bbuf3.at[slot], b3_sem, o, {"shard": z_peer(o) * 2 + core}
        )

    for o in range(1, nz):
        b3(o, zi).start()

    def add_source(src):
        select = jnp.where(touched_ref[...] == rows_ref[pl.ds(src, 1), :], 1.0, 0.0).astype(BF16)
        return jnp.dot(select, incoming[src], preferred_element_type=F32)

    rowacc[...] = add_source(shard)

    @pl.loop(1, n_shard)
    def _(o):
        a2a_in(o).wait_recv()
        rowacc[...] += add_source(shard_from(o))

    rowsend[...] = rowacc[...].astype(BF16)

    def rrs(o):
        target = rep_peer(o)
        r = pl.ds(pl.multiple_of(target * tblk, tblk), tblk)
        return remote(rowsend.at[r, :], rowbuf.at[o], rrs_sem, o, {"rep": target})

    for o in range(1, n_rep):
        rrs(o).start()

    for o in range(1, nz):
        p3(o).wait_recv()
    own_part = p2buf[0, pl.ds(pl.multiple_of(zi * zblk, zblk), zblk), :].astype(F32)
    for o in range(1, nz):
        own_part = own_part + p3buf[o].astype(F32)
    own_cols = pl.ds(pl.multiple_of(core * half, half), half)
    other_cols = pl.ds(pl.multiple_of((1 - core) * half, half), half)

    def z_rows(z):
        return pl.ds(pl.multiple_of(rep * rblk + z * zblk, zblk), zblk)

    wsum_ref[z_rows(zi), own_cols] = own_part.astype(BF16)

    def agz(o, z):
        place = wsum_ref.at[z_rows(z), own_cols]
        return remote(place, place, agz_sem, o, {"shard": z_peer(o) * 2 + core})

    for o in range(1, nz):
        agz(o, zi).start()

    for o in range(1, n_rep):
        rrs(o).wait_recv()
    mine = pl.ds(pl.multiple_of(rep * tblk, tblk), tblk)
    row_total = rowacc[mine, :]
    for o in range(1, n_rep):
        row_total = row_total + rowbuf[o].astype(F32)
    rowt_ref[mine, :] = row_total.astype(BF16)

    def rag(o, q):
        place = rowt_ref.at[pl.ds(pl.multiple_of(q * tblk, tblk), tblk), :]
        return remote(place, place, rag_sem, o, {"rep": rep_peer(o)})

    for o in range(1, n_rep):
        rag(o, rep).start()

    for o in range(1, nz):
        agz(o, z_from(o)).wait_recv()

    def rep_rows(q):
        return pl.ds(pl.multiple_of(q * rblk, rblk), rblk)

    def agr(o, q):
        place = wsum_ref.at[rep_rows(q), own_cols]
        return remote(place, place, agr_sem, o, {"rep": rep_peer(o)})

    def agc(o, q, cols):
        place = wsum_ref.at[rep_rows(q), cols]
        return remote(place, place, agc_sem, o, {"shard": partner})

    for o in range(1, n_rep):
        agr(o, rep).start()
    agc(0, rep, own_cols).start()

    for o in range(1, nz):
        b3(o, z_from(o)).wait_recv()
    bias_all = bbuf3[0]
    for z in range(1, nz):
        bias_all = bias_all + bbuf3[z]
    bsum_ref[...] = bias_all

    for o in range(1, n_rep):
        agr(o, rep_from(o)).wait_recv()
        agc(o, rep_from(o), own_cols).start()
    for o in range(1, n_rep):
        rag(o, rep_from(o)).wait_recv()
    for o in range(n_rep):
        agc(o, rep_from(o), other_cols).wait_recv()

    p1.wait_send()
    b1.wait_send()
    for o in range(1, n_rep):
        p2(o).wait_send()
        b2(o, rep).wait_send()
        rrs(o).wait_send()
        rag(o, rep).wait_send()
        agr(o, rep).wait_send()
    for o in range(1, nz):
        p3(o).wait_send()
        b3(o, zi).wait_send()
        agz(o, zi).wait_send()
    for o in range(n_rep):
        agc(o, rep_from(o), own_cols).wait_send()

    @pl.loop(1, n_shard)
    def _(o):
        a2a(o).wait_send()


def step_call(n_rep, n_shard, feats, cot, weight, cbias, code, rows, touched, width):
    tok, d = feats.shape
    nz = n_shard // 2
    slots = code.shape[1]
    count = touched.shape[0]
    half = d // 2
    rblk = d // n_rep
    zblk = rblk // nz
    tblk = count // n_rep
    vmem = pl.BlockSpec(memory_space=pltpu.VMEM)

    def sems(n):
        return pltpu.SemaphoreType.DMA((2, n))

    return pl.pallas_call(
        functools.partial(step_kernel, n_rep, n_shard),
        out_shape=(
            jax.ShapeDtypeStruct((d, d), BF16),
            jax.ShapeDtypeStruct((d // 128, 128), F32),
            jax.ShapeDtypeStruct((tok, width), BF16),
            jax.ShapeDtypeStruct((count, width), BF16),
        ),
        in_specs=[vmem] * 7,
        out_specs=(vmem,) * 4,
        scratch_shapes=[
            pltpu.VMEM((tok, d), BF16),
            pltpu.VMEM((tok, d), BF16),
            pltpu.VMEM((d, half), F32),
            pltpu.VMEM((d, half), BF16),
            pltpu.VMEM((d, half), BF16),
            pltpu.VMEM((d, half), BF16),
            pltpu.VMEM((n_rep, rblk, half), BF16),
            pltpu.VMEM((nz, zblk, half), BF16),
            pltpu.VMEM((2, d // 128, 128), F32),
            pltpu.VMEM((n_rep, d // 128, 128), F32),
            pltpu.VMEM((nz, d // 128, 128), F32),
            pltpu.VMEM((n_shard, slots, width), BF16),
            pltpu.VMEM((n_shard, slots, width), BF16),
            pltpu.VMEM((count, width), F32),
            pltpu.VMEM((count, width), BF16),
            pltpu.VMEM((n_rep, tblk, width), BF16),
            sems(1),
            sems(n_rep),
            sems(nz),
            sems(1),
            sems(n_rep),
            sems(nz),
            sems(n_shard),
            sems(n_rep),
            sems(n_rep),
            sems(nz),
            sems(n_rep),
            sems(n_rep),
        ],
        compiler_params=pltpu.CompilerParams(
            collective_id=0, has_side_effects=True, vmem_limit_bytes=56 * 1024 * 1024
        ),
    )(feats, cot, weight, cbias, code, rows, touched)


def adagrad_rows(table_rows, accum_rows, grads):
    new_accum = accum_rows + jnp.mean(grads * grads, axis=1)
    new_rows = keep_rate * table_rows - learn_rate * grads / jnp.sqrt(new_accum)[:, None]
    return (new_rows, new_accum)


def per_device(
    n_rep,
    n_shard,
    features,
    cotangent,
    cross_weight,
    cross_bias,
    emb_table,
    row_accum,
    send_bags,
    slot_counts,
    recv_rows,
    touched_rows,
):
    tok, d = features.shape
    shard_rows, width = emb_table.shape
    feats = d // width - 1
    scale = 1.0 / jnp.sqrt(F32(tok * n_rep * n_shard))
    bags = send_bags[0]
    live = jnp.arange(bags.shape[1], dtype=jnp.int32)[None, :] < slot_counts[0][:, None]
    code = jnp.where(live, (bags // feats) * 8 + bags % feats, -8)
    touched = touched_rows[0]
    weight_sum, bias_sum, dense_grad, rows = step_call(
        n_rep,
        n_shard,
        features,
        cotangent,
        cross_weight,
        cross_bias[None, :],
        code,
        recv_rows[0],
        touched[:, None],
        width,
    )
    weight_grad = weight_sum.astype(F32) * scale
    bias_grad = bias_sum.reshape(-1) * scale
    row_range = jnp.arange(shard_rows, dtype=jnp.int32)
    hit = row_range[:, None] == touched[None, :]
    marks = jnp.any(hit, axis=1)
    row_grads = jnp.dot(hit.astype(BF16), rows, preferred_element_type=F32)
    upd_table, upd_accum = adagrad_rows(emb_table, row_accum, row_grads)
    new_table = jnp.where(marks[:, None], upd_table, emb_table)
    new_accum = jnp.where(marks, upd_accum, row_accum)
    return (weight_grad, bias_grad, dense_grad, new_table, new_accum)


def solution(mesh):
    in_specs = (
        P(("rep", "shard"), None),
        P(("rep", "shard"), None),
        P(),
        P(),
        P("shard", None),
        P("shard"),
        P(("rep", "shard"), None, None),
        P(("rep", "shard"), None),
        P(("rep", "shard"), None, None),
        P("shard", None),
    )
    out_specs = (P(), P(), P(("rep", "shard"), None), P("shard", None), P("shard"))
    return jax.shard_map(
        functools.partial(per_device, mesh.shape["rep"], mesh.shape["shard"]),
        mesh=mesh,
        in_specs=in_specs,
        out_specs=out_specs,
        check_vma=False,
    )
```

```python
import functools
import math

import jax
import jax.numpy as jnp
from jax import lax
from jax.experimental import pallas as pl
from jax.experimental.pallas import tpu as pltpu
from jax.sharding import PartitionSpec as P

learn_rate = 0.5
keep_rate = 0.9
MESH = pl.DeviceIdType.MESH
F32 = jnp.float32
BF16 = jnp.bfloat16


def step_kernel(
    n_rep,
    n_shard,
    feat_ref,
    cot_ref,
    w_ref,
    cbias_ref,
    bags_ref,
    counts_ref,
    rows_ref,
    touched_ref,
    wsum_ref,
    bsum_ref,
    dense_ref,
    rowt_ref,
    gated,
    ig,
    feat_t,
    wown,
    wsend,
    wpair,
    p1buf,
    p2buf,
    p3buf,
    bbuf1,
    bbuf2,
    bbuf3,
    outgoing,
    incoming,
    touched_col,
    rowacc,
    rowsend,
    rowbuf,
    p1_sem,
    p2_sem,
    p3_sem,
    b1_sem,
    b2_sem,
    b3_sem,
    a2a_sem,
    rrs_sem,
    rag_sem,
    agz_sem,
    agr_sem,
    agc_sem,
):
    nz = n_shard // 2
    rep = lax.axis_index("rep")
    shard = lax.axis_index("shard")
    core = lax.rem(shard, 2)
    zi = shard // 2
    partner = zi * 2 + (1 - core)
    tok, d = feat_ref.shape
    width = dense_ref.shape[1]
    feats = d // width - 1
    half = d // 2
    parts = half // 128
    rblk = d // n_rep
    zblk = rblk // nz
    touched_count = rowt_ref.shape[0]
    tblk = touched_count // n_rep
    slots = bags_ref.shape[1]
    inverse = (1 << 16) // feats + 1
    assert tok * feats * (inverse * feats - (1 << 16)) < 1 << 16

    def rep_peer(o):
        return lax.rem(rep + o, n_rep)

    def rep_from(o):
        return lax.rem(rep + n_rep - o, n_rep)

    def z_peer(o):
        return lax.rem(zi + o, nz)

    def z_from(o):
        return lax.rem(zi + nz - o, nz)

    def shard_peer(o):
        return lax.rem(shard + o, n_shard)

    def shard_from(o):
        return lax.rem(shard + n_shard - o, n_shard)

    def remote(src, dst, sems, index, target):
        return pltpu.make_async_remote_copy(
            src_ref=src,
            dst_ref=dst,
            send_sem=sems.at[0, index],
            recv_sem=sems.at[1, index],
            device_id=target,
            device_id_type=MESH,
        )

    def rep_rows(q):
        return pl.ds(pl.multiple_of(q * rblk, rblk), rblk)

    def z_rows(z):
        return pl.ds(pl.multiple_of(z * zblk, zblk), zblk)

    barrier = pltpu.get_barrier_semaphore()
    for o in range(1, n_shard):
        pl.semaphore_signal(
            barrier, inc=1, device_id={"shard": shard_peer(o)}, device_id_type=MESH
        )
    for o in range(1, n_rep):
        pl.semaphore_signal(barrier, inc=1, device_id={"rep": rep_peer(o)}, device_id_type=MESH)

    @pl.loop(0, tok // 128)
    def _(i):
        r = pl.ds(pl.multiple_of(i * 128, 128), 128)
        gated[r, :] = (cot_ref[r, :].astype(F32) * feat_ref[r, :].astype(F32)).astype(BF16)

    @pl.loop(0, d // 256)
    def _(i):
        r = pl.ds(pl.multiple_of(i * 256, 256), 256)
        feat_t[r, :] = jnp.transpose(feat_ref[:, r])

    def weight_pair(col_half, j, out, out_type):
        cols = pl.ds(pl.multiple_of(col_half * half + j * 256, 256), 256)

        @pl.loop(0, d // 256)
        def _(i):
            r = pl.ds(pl.multiple_of(i * 256, 256), 256)
            terms = jnp.dot(feat_t[r, :], gated[:, cols], preferred_element_type=F32)
            out[2 * j, r, :] = terms[:, :128].astype(out_type)
            out[2 * j + 1, r, :] = terms[:, 128:].astype(out_type)

    def p1(k):
        return remote(wsend.at[k], p1buf.at[k], p1_sem, k, {"shard": partner})

    for j in range(parts // 2):
        weight_pair(1 - core, j, wsend, BF16)
        if j == 0:
            pl.semaphore_wait(barrier, n_shard - 1 + n_rep - 1)
        p1(2 * j).start()
        p1(2 * j + 1).start()

    def p2(k, o):
        target = rep_peer(o)
        return remote(
            wpair.at[k, rep_rows(target), :],
            p2buf.at[k, o],
            p2_sem,
            k * n_rep + o,
            {"rep": target},
        )

    for j in range(parts // 2):
        weight_pair(core, j, wown, F32)
        for k in (2 * j, 2 * j + 1):
            p1(k).wait_recv()

            @pl.loop(0, n_rep)
            def _(i):
                r = rep_rows(i)
                wpair[k, r, :] = (wown[k, r, :] + p1buf[k, r, :].astype(F32)).astype(BF16)

            for o in range(1, n_rep):
                p2(k, o).start()

    bias_row = jnp.sum(gated[...].astype(F32), axis=0, keepdims=True)
    for j in range(d // 128):
        bbuf1[0, pl.ds(j, 1), :] = bias_row[:, j * 128 : (j + 1) * 128]
    b1 = remote(bbuf1.at[0], bbuf1.at[1], b1_sem, 0, {"shard": partner})
    b1.start()

    @pl.loop(0, d // 256)
    def _(i):
        c = pl.ds(pl.multiple_of(i * 256, 256), 256)
        linear = jnp.dot(feat_ref[...], w_ref[:, c], preferred_element_type=F32) + cbias_ref[:, c]
        back = lax.dot_general(
            gated[...], w_ref[c, :], (((1,), (1,)), ((), ())), preferred_element_type=F32
        )
        cot = cot_ref[:, c].astype(F32)
        ig[:, c] = (cot * linear + back + cot).astype(BF16)

    b1.wait_recv()
    bbuf2[rep] = bbuf1[0] + bbuf1[1]

    def b2(o, slot):
        return remote(bbuf2.at[slot], bbuf2.at[slot], b2_sem, o, {"rep": rep_peer(o)})

    for o in range(1, n_rep):
        b2(o, rep).start()

    def gather(dest):
        bags = bags_ref[pl.ds(dest, 1), :]
        place = lax.broadcasted_iota(jnp.int32, (1, slots), 1)
        sample = jnp.right_shift(bags * inverse, 16)
        code = jnp.where(place < counts_ref[0, dest], sample * 8 + (bags - sample * feats), -8)
        code = jnp.transpose(jnp.broadcast_to(code, (128, slots)))
        sample = jnp.right_shift(code, 3)
        feature = jnp.bitwise_and(code, 7)
        lane = lax.broadcasted_iota(jnp.int32, (slots, 128), 1)
        select = jnp.concatenate(
            [jnp.where(sample == lane + k * 128, 1.0, 0.0) for k in range(tok // 128)], axis=1
        ).astype(BF16)
        wide = jnp.dot(select, ig[:, width:], preferred_element_type=F32)
        picked = jnp.zeros((slots, width), F32)
        for f in range(feats):
            picked = jnp.where(feature == f, wide[:, f * width : (f + 1) * width], picked)
        return picked.astype(BF16)

    def a2a(o):
        dest = shard_peer(o)
        return remote(outgoing.at[dest], incoming.at[shard], a2a_sem, o, {"shard": dest})

    def a2a_in(o):
        src = shard_from(o)
        return remote(outgoing.at[src], incoming.at[src], a2a_sem, o, {"shard": src})

    @pl.loop(1, n_shard)
    def _(o):
        outgoing[shard_peer(o)] = gather(shard_peer(o))
        a2a(o).start()

    incoming[shard] = gather(shard)
    dense_ref[...] = ig[:, :width]
    touched_col[...] = jnp.transpose(
        jnp.broadcast_to(touched_ref[...], (128, touched_count))
    )

    def p3(k, o):
        target = z_peer(o)
        return remote(
            p2buf.at[k, 0, z_rows(target), :],
            p3buf.at[k, o],
            p3_sem,
            k * nz + o,
            {"shard": target * 2 + core},
        )

    def agz(k, o, z):
        place = wsum_ref.at[
            core * parts + k, pl.ds(pl.multiple_of(rep * rblk + z * zblk, zblk), zblk), :
        ]
        return remote(place, place, agz_sem, k * nz + o, {"shard": z_peer(o) * 2 + core})

    def agr(k, o, q):
        place = wsum_ref.at[core * parts + k, rep_rows(q), :]
        return remote(place, place, agr_sem, k * n_rep + o, {"rep": rep_peer(o)})

    def agc(k, o, q, side):
        place = wsum_ref.at[side * parts + k, rep_rows(q), :]
        return remote(place, place, agc_sem, k * n_rep + o, {"shard": partner})

    for t in range(parts + 2):
        if t < parts:
            k = t
            for o in range(1, n_rep):
                p2(k, o).wait_recv()
            total = wpair[k, rep_rows(rep), :].astype(F32)
            for o in range(1, n_rep):
                total = total + p2buf[k, o].astype(F32)
            p2buf[k, 0] = total.astype(BF16)
            for o in range(1, nz):
                p3(k, o).start()
        if 1 <= t <= parts:
            k = t - 1
            for o in range(1, nz):
                p3(k, o).wait_recv()
            block = p2buf[k, 0, z_rows(zi), :].astype(F32)
            for o in range(1, nz):
                block = block + p3buf[k, o].astype(F32)
            mine = pl.ds(pl.multiple_of(rep * rblk + zi * zblk, zblk), zblk)
            wsum_ref[core * parts + k, mine, :] = block.astype(BF16)
            for o in range(1, nz):
                agz(k, o, zi).start()
        if 2 <= t:
            k = t - 2
            for o in range(1, nz):
                agz(k, o, z_from(o)).wait_recv()
            for o in range(1, n_rep):
                agr(k, o, rep).start()
            agc(k, 0, rep, core).start()

    for o in range(1, n_rep):
        b2(o, rep_from(o)).wait_recv()
    bias_rep = bbuf2[0]
    for q in range(1, n_rep):
        bias_rep = bias_rep + bbuf2[q]
    bbuf3[zi] = bias_rep

    def b3(o, slot):
        return remote(
            bbuf3.at[slot], bbuf3.at[slot], b3_sem, o, {"shard": z_peer(o) * 2 + core}
        )

    for o in range(1, nz):
        b3(o, zi).start()

    def add_source(src):
        rows = rows_ref[pl.ds(src, 1), :]
        select = jnp.concatenate(
            [
                jnp.where(touched_col[...] == rows[:, k * 128 : (k + 1) * 128], 1.0, 0.0)
                for k in range(slots // 128)
            ],
            axis=1,
        ).astype(BF16)
        return jnp.dot(select, incoming[src], preferred_element_type=F32)

    rowacc[...] = add_source(shard)

    @pl.loop(1, n_shard)
    def _(o):
        a2a_in(o).wait_recv()
        rowacc[...] += add_source(shard_from(o))

    rowsend[...] = rowacc[...].astype(BF16)

    def rrs(o):
        target = rep_peer(o)
        r = pl.ds(pl.multiple_of(target * tblk, tblk), tblk)
        return remote(rowsend.at[r, :], rowbuf.at[o], rrs_sem, o, {"rep": target})

    for o in range(1, n_rep):
        rrs(o).start()

    for k in range(parts // 2):
        for o in range(1, n_rep):
            agr(k, o, rep_from(o)).wait_recv()
            agc(k, o, rep_from(o), core).start()

    for o in range(1, n_rep):
        rrs(o).wait_recv()
    own = pl.ds(pl.multiple_of(rep * tblk, tblk), tblk)
    row_total = rowacc[own, :]
    for o in range(1, n_rep):
        row_total = row_total + rowbuf[o].astype(F32)
    rowt_ref[own, :] = row_total.astype(BF16)

    def rag(o, q):
        place = rowt_ref.at[pl.ds(pl.multiple_of(q * tblk, tblk), tblk), :]
        return remote(place, place, rag_sem, o, {"rep": rep_peer(o)})

    for o in range(1, n_rep):
        rag(o, rep).start()

    for o in range(1, nz):
        b3(o, z_from(o)).wait_recv()
    bias_all = bbuf3[0]
    for z in range(1, nz):
        bias_all = bias_all + bbuf3[z]
    bsum_ref[...] = bias_all

    for k in range(parts // 2, parts):
        for o in range(1, n_rep):
            agr(k, o, rep_from(o)).wait_recv()
            agc(k, o, rep_from(o), core).start()
    for o in range(1, n_rep):
        rag(o, rep_from(o)).wait_recv()
    for k in range(parts):
        for o in range(n_rep):
            agc(k, o, rep_from(o), 1 - core).wait_recv()

    b1.wait_send()
    for o in range(1, n_rep):
        b2(o, rep).wait_send()
        rrs(o).wait_send()
        rag(o, rep).wait_send()
    for o in range(1, nz):
        b3(o, zi).wait_send()
    for k in range(parts):
        p1(k).wait_send()
        for o in range(1, n_rep):
            p2(k, o).wait_send()
            agr(k, o, rep).wait_send()
        for o in range(1, nz):
            p3(k, o).wait_send()
            agz(k, o, zi).wait_send()
        for o in range(n_rep):
            agc(k, o, rep_from(o), core).wait_send()

    @pl.loop(1, n_shard)
    def _(o):
        a2a(o).wait_send()


def step_call(n_rep, n_shard, feats, cot, weight, cbias, bags, counts, rows, touched, width):
    tok, d = feats.shape
    nz = n_shard // 2
    slots = bags.shape[1]
    count = touched.shape[1]
    half = d // 2
    parts = half // 128
    rblk = d // n_rep
    zblk = rblk // nz
    tblk = count // n_rep
    vmem = pl.BlockSpec(memory_space=pltpu.VMEM)
    smem = pl.BlockSpec(memory_space=pltpu.SMEM)

    def sems(n):
        return pltpu.SemaphoreType.DMA((2, n))

    return pl.pallas_call(
        functools.partial(step_kernel, n_rep, n_shard),
        out_shape=(
            jax.ShapeDtypeStruct((2 * parts, d, 128), BF16),
            jax.ShapeDtypeStruct((d // 128, 128), F32),
            jax.ShapeDtypeStruct((tok, width), BF16),
            jax.ShapeDtypeStruct((count, width), BF16),
        ),
        in_specs=[vmem] * 5 + [smem] + [vmem] * 2,
        out_specs=(vmem,) * 4,
        scratch_shapes=[
            pltpu.VMEM((tok, d), BF16),
            pltpu.VMEM((tok, d), BF16),
            pltpu.VMEM((d, tok), BF16),
            pltpu.VMEM((parts, d, 128), F32),
            pltpu.VMEM((parts, d, 128), BF16),
            pltpu.VMEM((parts, d, 128), BF16),
            pltpu.VMEM((parts, d, 128), BF16),
            pltpu.VMEM((parts, n_rep, rblk, 128), BF16),
            pltpu.VMEM((parts, nz, zblk, 128), BF16),
            pltpu.VMEM((2, d // 128, 128), F32),
            pltpu.VMEM((n_rep, d // 128, 128), F32),
            pltpu.VMEM((nz, d // 128, 128), F32),
            pltpu.VMEM((n_shard, slots, width), BF16),
            pltpu.VMEM((n_shard, slots, width), BF16),
            pltpu.VMEM((count, 128), jnp.int32),
            pltpu.VMEM((count, width), F32),
            pltpu.VMEM((count, width), BF16),
            pltpu.VMEM((n_rep, tblk, width), BF16),
            sems(parts),
            sems(parts * n_rep),
            sems(parts * nz),
            sems(1),
            sems(n_rep),
            sems(nz),
            sems(n_shard),
            sems(n_rep),
            sems(n_rep),
            sems(parts * nz),
            sems(parts * n_rep),
            sems(parts * n_rep),
        ],
        compiler_params=pltpu.CompilerParams(
            collective_id=0, has_side_effects=True, vmem_limit_bytes=56 * 1024 * 1024
        ),
    )(feats, cot, weight, cbias, bags, counts, rows, touched)


def update_kernel(
    scale,
    wsum_ref,
    bsum_ref,
    dense_ref,
    rowt_ref,
    touched_ref,
    accum_ref,
    table_ref,
    wgrad_ref,
    bgrad_ref,
    dense_out_ref,
    accum_out_ref,
    table_out_ref,
):
    step = pl.program_id(0)
    count, width = rowt_ref.shape
    for c in range(wsum_ref.shape[0]):
        wgrad_ref[:, c * 128 : (c + 1) * 128] = wsum_ref[c].astype(F32) * scale
    dense_out_ref[...] = dense_ref[...]
    bgrad_ref[...] = bsum_ref[...] * scale

    source = jnp.concatenate([rowt_ref[...], jnp.ones((count, 128), BF16)], axis=1)
    blocks = table_ref.shape[0] // 128
    for i in range(blocks):
        block = step * blocks + i
        row_ids = block * 128 + lax.broadcasted_iota(jnp.int32, (128, count), 0)
        select = jnp.where(row_ids == touched_ref[...], 1.0, 0.0).astype(BF16)
        spread = jnp.dot(select, source, preferred_element_type=F32)
        grads = spread[:, :width]
        flipped = jnp.transpose(grads)
        square = jnp.sum(flipped * flipped, axis=0, keepdims=True)
        new_accum = accum_ref[pl.ds(block, 1), :] + square / width
        accum_out_ref[pl.ds(block, 1), :] = new_accum
        rate = jnp.transpose(jnp.broadcast_to(learn_rate / jnp.sqrt(new_accum), (width, 128)))
        r = pl.ds(i * 128, 128)
        rows = table_ref[r, :]
        table_out_ref[r, :] = jnp.where(
            spread[:, width:] > 0.5, keep_rate * rows - grads * rate, rows
        )


def update_call(scale, wsum, bsum, dense, rowt, touched, accum, table):
    pieces, d, _ = wsum.shape
    tok, width = dense.shape
    count = rowt.shape[0]
    shard_rows = table.shape[0]
    steps = 8

    def whole(shape):
        return pl.BlockSpec(shape, lambda i: (0,) * len(shape))

    return pl.pallas_call(
        functools.partial(update_kernel, scale),
        grid=(steps,),
        in_specs=[
            pl.BlockSpec((pieces, d // steps, 128), lambda i: (0, i, 0)),
            whole(bsum.shape),
            pl.BlockSpec((tok // steps, width), lambda i: (i, 0)),
            whole((count, width)),
            whole((1, count)),
            whole(accum.shape),
            pl.BlockSpec((shard_rows // steps, width), lambda i: (i, 0)),
        ],
        out_specs=(
            pl.BlockSpec((d // steps, d), lambda i: (i, 0)),
            whole(bsum.shape),
            pl.BlockSpec((tok // steps, width), lambda i: (i, 0)),
            whole(accum.shape),
            pl.BlockSpec((shard_rows // steps, width), lambda i: (i, 0)),
        ),
        out_shape=(
            jax.ShapeDtypeStruct((d, d), F32),
            jax.ShapeDtypeStruct(bsum.shape, F32),
            jax.ShapeDtypeStruct((tok, width), BF16),
            jax.ShapeDtypeStruct(accum.shape, F32),
            jax.ShapeDtypeStruct(table.shape, F32),
        ),
        compiler_params=pltpu.CompilerParams(vmem_limit_bytes=40 * 1024 * 1024),
    )(wsum, bsum, dense, rowt, touched, accum, table)


def per_device(
    n_rep,
    n_shard,
    features,
    cotangent,
    cross_weight,
    cross_bias,
    emb_table,
    row_accum,
    send_bags,
    slot_counts,
    recv_rows,
    touched_rows,
):
    tok = features.shape[0]
    width = emb_table.shape[1]
    scale = 1.0 / math.sqrt(tok * n_rep * n_shard)
    weight_sum, bias_sum, dense, rows = step_call(
        n_rep,
        n_shard,
        features,
        cotangent,
        cross_weight,
        cross_bias[None, :],
        send_bags[0],
        slot_counts,
        recv_rows[0],
        touched_rows,
        width,
    )
    weight_grad, bias_grad, dense_grad, new_accum, new_table = update_call(
        scale, weight_sum, bias_sum, dense, rows, touched_rows, row_accum.reshape(-1, 128), emb_table
    )
    return (weight_grad, bias_grad.reshape(-1), dense_grad, new_table, new_accum.reshape(-1))


def solution(mesh):
    in_specs = (
        P(("rep", "shard"), None),
        P(("rep", "shard"), None),
        P(),
        P(),
        P("shard", None),
        P("shard"),
        P(("rep", "shard"), None, None),
        P(("rep", "shard"), None),
        P(("rep", "shard"), None, None),
        P("shard", None),
    )
    out_specs = (P(), P(), P(("rep", "shard"), None), P("shard", None), P("shard"))
    return jax.shard_map(
        functools.partial(per_device, mesh.shape["rep"], mesh.shape["shard"]),
        mesh=mesh,
        in_specs=in_specs,
        out_specs=out_specs,
        check_vma=False,
    )
```

```python
import functools
import math

import jax
import jax.numpy as jnp
from jax import lax
from jax.experimental import pallas as pl
from jax.experimental.pallas import tpu as pltpu
from jax.sharding import PartitionSpec as P

learn_rate = 0.5
keep_rate = 0.9
MESH = pl.DeviceIdType.MESH
F32 = jnp.float32
BF16 = jnp.bfloat16


def step_kernel(
    n_rep,
    n_shard,
    feat_ref,
    cot_ref,
    w_hbm,
    cbias_ref,
    bags_ref,
    counts_ref,
    rows_ref,
    touched_ref,
    wsum_hbm,
    bsum_ref,
    dense_ref,
    rowt_ref,
    w_ref,
    wsum_ref,
    gated,
    ig,
    feat_t,
    wown,
    wsend,
    wpair,
    p1buf,
    p2buf,
    p3buf,
    bbuf1,
    bbuf2,
    bbuf3,
    outgoing,
    incoming,
    touched_col,
    rowacc,
    rowsend,
    rowbuf,
    p1_sem,
    p2_sem,
    p3_sem,
    b1_sem,
    b2_sem,
    b3_sem,
    a2a_sem,
    rrs_sem,
    rag_sem,
    agz_sem,
    agr_sem,
    agc_sem,
    w_sem,
    out_sem,
):
    nz = n_shard // 2
    rep = lax.axis_index("rep")
    shard = lax.axis_index("shard")
    core = lax.rem(shard, 2)
    zi = shard // 2
    partner = zi * 2 + (1 - core)
    tok, d = feat_ref.shape
    width = dense_ref.shape[1]
    feats = d // width - 1
    half = d // 2
    parts = half // 128
    rblk = d // n_rep
    zblk = rblk // nz
    touched_count = rowt_ref.shape[0]
    tblk = touched_count // n_rep
    slots = bags_ref.shape[1]
    inverse = (1 << 16) // feats + 1
    assert tok * feats * (inverse * feats - (1 << 16)) < 1 << 16

    def rep_peer(o):
        return lax.rem(rep + o, n_rep)

    def rep_from(o):
        return lax.rem(rep + n_rep - o, n_rep)

    def z_peer(o):
        return lax.rem(zi + o, nz)

    def z_from(o):
        return lax.rem(zi + nz - o, nz)

    def shard_peer(o):
        return lax.rem(shard + o, n_shard)

    def shard_from(o):
        return lax.rem(shard + n_shard - o, n_shard)

    def remote(src, dst, sems, index, target):
        return pltpu.make_async_remote_copy(
            src_ref=src,
            dst_ref=dst,
            send_sem=sems.at[0, index],
            recv_sem=sems.at[1, index],
            device_id=target,
            device_id_type=MESH,
        )

    def rep_rows(q):
        return pl.ds(pl.multiple_of(q * rblk, rblk), rblk)

    def z_rows(z):
        return pl.ds(pl.multiple_of(z * zblk, zblk), zblk)

    w_copy = pltpu.make_async_copy(w_hbm, w_ref, w_sem.at[0])
    w_copy.start()
    barrier = pltpu.get_barrier_semaphore()
    for o in range(1, n_shard):
        pl.semaphore_signal(
            barrier, inc=1, device_id={"shard": shard_peer(o)}, device_id_type=MESH
        )
    for o in range(1, n_rep):
        pl.semaphore_signal(barrier, inc=1, device_id={"rep": rep_peer(o)}, device_id_type=MESH)

    @pl.loop(0, tok // 128)
    def _(i):
        r = pl.ds(pl.multiple_of(i * 128, 128), 128)
        gated[r, :] = (cot_ref[r, :].astype(F32) * feat_ref[r, :].astype(F32)).astype(BF16)

    @pl.loop(0, d // 256)
    def _(i):
        r = pl.ds(pl.multiple_of(i * 256, 256), 256)
        feat_t[r, :] = jnp.transpose(feat_ref[:, r])

    def weight_pair(col_half, j, out, out_type):
        cols = pl.ds(pl.multiple_of(col_half * half + j * 256, 256), 256)

        @pl.loop(0, d // 256)
        def _(i):
            r = pl.ds(pl.multiple_of(i * 256, 256), 256)
            terms = jnp.dot(feat_t[r, :], gated[:, cols], preferred_element_type=F32)
            out[2 * j, r, :] = terms[:, :128].astype(out_type)
            out[2 * j + 1, r, :] = terms[:, 128:].astype(out_type)

    def p1(k):
        return remote(wsend.at[k], p1buf.at[k], p1_sem, k, {"shard": partner})

    for j in range(parts // 2):
        weight_pair(1 - core, j, wsend, BF16)
        if j == 0:
            pl.semaphore_wait(barrier, n_shard - 1 + n_rep - 1)
        p1(2 * j).start()
        p1(2 * j + 1).start()

    def p2(k, o):
        target = rep_peer(o)
        return remote(
            wpair.at[k, rep_rows(target), :],
            p2buf.at[k, o],
            p2_sem,
            k * n_rep + o,
            {"rep": target},
        )

    for j in range(parts // 2):
        weight_pair(core, j, wown, F32)
        for k in (2 * j, 2 * j + 1):
            p1(k).wait_recv()

            @pl.loop(0, n_rep)
            def _(i):
                r = rep_rows(i)
                wpair[k, r, :] = (wown[k, r, :] + p1buf[k, r, :].astype(F32)).astype(BF16)

            for o in range(1, n_rep):
                p2(k, o).start()

    bias_row = jnp.sum(gated[...].astype(F32), axis=0, keepdims=True)
    for j in range(d // 128):
        bbuf1[0, pl.ds(j, 1), :] = bias_row[:, j * 128 : (j + 1) * 128]
    b1 = remote(bbuf1.at[0], bbuf1.at[1], b1_sem, 0, {"shard": partner})
    b1.start()

    w_copy.wait()

    @pl.loop(0, d // 256)
    def _(i):
        c = pl.ds(pl.multiple_of(i * 256, 256), 256)
        linear = jnp.dot(feat_ref[...], w_ref[:, c], preferred_element_type=F32) + cbias_ref[:, c]
        back = lax.dot_general(
            gated[...], w_ref[c, :], (((1,), (1,)), ((), ())), preferred_element_type=F32
        )
        cot = cot_ref[:, c].astype(F32)
        ig[:, c] = (cot * linear + back + cot).astype(BF16)

    b1.wait_recv()
    bbuf2[rep] = bbuf1[0] + bbuf1[1]

    def b2(o, slot):
        return remote(bbuf2.at[slot], bbuf2.at[slot], b2_sem, o, {"rep": rep_peer(o)})

    for o in range(1, n_rep):
        b2(o, rep).start()

    def gather(dest):
        bags = bags_ref[pl.ds(dest, 1), :]
        place = lax.broadcasted_iota(jnp.int32, (1, slots), 1)
        sample = jnp.right_shift(bags * inverse, 16)
        code = jnp.where(place < counts_ref[0, dest], sample * 8 + (bags - sample * feats), -8)
        code = jnp.transpose(jnp.broadcast_to(code, (128, slots)))
        sample = jnp.right_shift(code, 3)
        feature = jnp.bitwise_and(code, 7)
        lane = lax.broadcasted_iota(jnp.int32, (slots, 128), 1)
        select = jnp.concatenate(
            [jnp.where(sample == lane + k * 128, 1.0, 0.0) for k in range(tok // 128)], axis=1
        ).astype(BF16)
        wide = jnp.dot(select, ig[:, width:], preferred_element_type=F32)
        picked = jnp.zeros((slots, width), F32)
        for f in range(feats):
            picked = jnp.where(feature == f, wide[:, f * width : (f + 1) * width], picked)
        return picked.astype(BF16)

    def a2a(o):
        dest = shard_peer(o)
        return remote(outgoing.at[dest], incoming.at[shard], a2a_sem, o, {"shard": dest})

    def a2a_in(o):
        src = shard_from(o)
        return remote(outgoing.at[src], incoming.at[src], a2a_sem, o, {"shard": src})

    def send_slots(low, high):
        @pl.loop(low, high)
        def _(o):
            outgoing[shard_peer(o)] = gather(shard_peer(o))
            a2a(o).start()

    def p3(k, o):
        target = z_peer(o)
        return remote(
            p2buf.at[k, 0, z_rows(target), :],
            p3buf.at[k, o],
            p3_sem,
            k * nz + o,
            {"shard": target * 2 + core},
        )

    def agz(k, o, z):
        place = wsum_ref.at[
            core * parts + k, pl.ds(pl.multiple_of(rep * rblk + z * zblk, zblk), zblk), :
        ]
        return remote(place, place, agz_sem, k * nz + o, {"shard": z_peer(o) * 2 + core})

    def agr(k, o, q):
        place = wsum_ref.at[core * parts + k, rep_rows(q), :]
        return remote(place, place, agr_sem, k * n_rep + o, {"rep": rep_peer(o)})

    def agc(k, o, q, side):
        place = wsum_ref.at[side * parts + k, rep_rows(q), :]
        return remote(place, place, agc_sem, k * n_rep + o, {"shard": partner})

    cuts = (1, n_shard // 2 - 1, n_shard - 2, n_shard)
    for t in range(parts + 2):
        if t < parts:
            k = t
            for o in range(1, n_rep):
                p2(k, o).wait_recv()
            total = wpair[k, rep_rows(rep), :].astype(F32)
            for o in range(1, n_rep):
                total = total + p2buf[k, o].astype(F32)
            p2buf[k, 0] = total.astype(BF16)
            for o in range(1, nz):
                p3(k, o).start()
            if t < 3:
                send_slots(cuts[t], cuts[t + 1])
        if 1 <= t <= parts:
            k = t - 1
            for o in range(1, nz):
                p3(k, o).wait_recv()
            block = p2buf[k, 0, z_rows(zi), :].astype(F32)
            for o in range(1, nz):
                block = block + p3buf[k, o].astype(F32)
            mine = pl.ds(pl.multiple_of(rep * rblk + zi * zblk, zblk), zblk)
            wsum_ref[core * parts + k, mine, :] = block.astype(BF16)
            for o in range(1, nz):
                agz(k, o, zi).start()
        if 2 <= t:
            k = t - 2
            for o in range(1, nz):
                agz(k, o, z_from(o)).wait_recv()
            for o in range(1, n_rep):
                agr(k, o, rep).start()
            agc(k, 0, rep, core).start()

    incoming[shard] = gather(shard)
    dense_ref[...] = ig[:, :width]
    touched_col[...] = jnp.transpose(
        jnp.broadcast_to(touched_ref[...], (128, touched_count))
    )
    for o in range(1, n_rep):
        b2(o, rep_from(o)).wait_recv()
    bias_rep = bbuf2[0]
    for q in range(1, n_rep):
        bias_rep = bias_rep + bbuf2[q]
    bbuf3[zi] = bias_rep

    def b3(o, slot):
        return remote(
            bbuf3.at[slot], bbuf3.at[slot], b3_sem, o, {"shard": z_peer(o) * 2 + core}
        )

    for o in range(1, nz):
        b3(o, zi).start()

    def add_source(src):
        rows = rows_ref[pl.ds(src, 1), :]
        select = jnp.concatenate(
            [
                jnp.where(touched_col[...] == rows[:, k * 128 : (k + 1) * 128], 1.0, 0.0)
                for k in range(slots // 128)
            ],
            axis=1,
        ).astype(BF16)
        return jnp.dot(select, incoming[src], preferred_element_type=F32)

    rowacc[...] = add_source(shard)

    @pl.loop(1, n_shard)
    def _(o):
        a2a_in(o).wait_recv()
        rowacc[...] += add_source(shard_from(o))

    rowsend[...] = rowacc[...].astype(BF16)

    def rrs(o):
        target = rep_peer(o)
        r = pl.ds(pl.multiple_of(target * tblk, tblk), tblk)
        return remote(rowsend.at[r, :], rowbuf.at[o], rrs_sem, o, {"rep": target})

    for o in range(1, n_rep):
        rrs(o).start()

    def write_out(side, k):
        piece = side * parts + k
        return pltpu.make_async_copy(wsum_ref.at[piece], wsum_hbm.at[piece], out_sem.at[piece])

    for k in range(parts // 2):
        for o in range(1, n_rep):
            agr(k, o, rep_from(o)).wait_recv()
            agc(k, o, rep_from(o), core).start()
        write_out(core, k).start()

    for o in range(1, n_rep):
        rrs(o).wait_recv()
    own = pl.ds(pl.multiple_of(rep * tblk, tblk), tblk)
    row_total = rowacc[own, :]
    for o in range(1, n_rep):
        row_total = row_total + rowbuf[o].astype(F32)
    rowt_ref[own, :] = row_total.astype(BF16)

    def rag(o, q):
        place = rowt_ref.at[pl.ds(pl.multiple_of(q * tblk, tblk), tblk), :]
        return remote(place, place, rag_sem, o, {"rep": rep_peer(o)})

    for o in range(1, n_rep):
        rag(o, rep).start()

    for o in range(1, nz):
        b3(o, z_from(o)).wait_recv()
    bias_all = bbuf3[0]
    for z in range(1, nz):
        bias_all = bias_all + bbuf3[z]
    bsum_ref[...] = bias_all

    for k in range(parts // 2, parts):
        for o in range(1, n_rep):
            agr(k, o, rep_from(o)).wait_recv()
            agc(k, o, rep_from(o), core).start()
        write_out(core, k).start()
    for o in range(1, n_rep):
        rag(o, rep_from(o)).wait_recv()
    for k in range(parts):
        for o in range(n_rep):
            agc(k, o, rep_from(o), 1 - core).wait_recv()
        write_out(1 - core, k).start()

    b1.wait_send()
    for o in range(1, n_rep):
        b2(o, rep).wait_send()
        rrs(o).wait_send()
        rag(o, rep).wait_send()
    for o in range(1, nz):
        b3(o, zi).wait_send()
    for k in range(parts):
        p1(k).wait_send()
        for o in range(1, n_rep):
            p2(k, o).wait_send()
            agr(k, o, rep).wait_send()
        for o in range(1, nz):
            p3(k, o).wait_send()
            agz(k, o, zi).wait_send()
        for o in range(n_rep):
            agc(k, o, rep_from(o), core).wait_send()
        write_out(core, k).wait()
        write_out(1 - core, k).wait()

    @pl.loop(1, n_shard)
    def _(o):
        a2a(o).wait_send()


def step_call(n_rep, n_shard, feats, cot, weight, cbias, bags, counts, rows, touched, width):
    tok, d = feats.shape
    nz = n_shard // 2
    slots = bags.shape[1]
    count = touched.shape[1]
    half = d // 2
    parts = half // 128
    rblk = d // n_rep
    zblk = rblk // nz
    tblk = count // n_rep
    vmem = pl.BlockSpec(memory_space=pltpu.VMEM)
    smem = pl.BlockSpec(memory_space=pltpu.SMEM)
    hbm = pl.BlockSpec(memory_space=pl.ANY)

    def sems(n):
        return pltpu.SemaphoreType.DMA((2, n))

    return pl.pallas_call(
        functools.partial(step_kernel, n_rep, n_shard),
        out_shape=(
            jax.ShapeDtypeStruct((2 * parts, d, 128), BF16),
            jax.ShapeDtypeStruct((d // 128, 128), F32),
            jax.ShapeDtypeStruct((tok, width), BF16),
            jax.ShapeDtypeStruct((count, width), BF16),
        ),
        in_specs=[vmem, vmem, hbm, vmem, vmem, smem, vmem, vmem],
        out_specs=(hbm, vmem, vmem, vmem),
        scratch_shapes=[
            pltpu.VMEM((d, d), BF16),
            pltpu.VMEM((2 * parts, d, 128), BF16),
            pltpu.VMEM((tok, d), BF16),
            pltpu.VMEM((tok, d), BF16),
            pltpu.VMEM((d, tok), BF16),
            pltpu.VMEM((parts, d, 128), F32),
            pltpu.VMEM((parts, d, 128), BF16),
            pltpu.VMEM((parts, d, 128), BF16),
            pltpu.VMEM((parts, d, 128), BF16),
            pltpu.VMEM((parts, n_rep, rblk, 128), BF16),
            pltpu.VMEM((parts, nz, zblk, 128), BF16),
            pltpu.VMEM((2, d // 128, 128), F32),
            pltpu.VMEM((n_rep, d // 128, 128), F32),
            pltpu.VMEM((nz, d // 128, 128), F32),
            pltpu.VMEM((n_shard, slots, width), BF16),
            pltpu.VMEM((n_shard, slots, width), BF16),
            pltpu.VMEM((count, 128), jnp.int32),
            pltpu.VMEM((count, width), F32),
            pltpu.VMEM((count, width), BF16),
            pltpu.VMEM((n_rep, tblk, width), BF16),
            sems(parts),
            sems(parts * n_rep),
            sems(parts * nz),
            sems(1),
            sems(n_rep),
            sems(nz),
            sems(n_shard),
            sems(n_rep),
            sems(n_rep),
            sems(parts * nz),
            sems(parts * n_rep),
            sems(parts * n_rep),
            pltpu.SemaphoreType.DMA((1,)),
            pltpu.SemaphoreType.DMA((2 * parts,)),
        ],
        compiler_params=pltpu.CompilerParams(
            collective_id=0, has_side_effects=True, vmem_limit_bytes=60 * 1024 * 1024
        ),
    )(feats, cot, weight, cbias, bags, counts, rows, touched)


def update_kernel(
    scale,
    wsum_ref,
    bsum_ref,
    dense_ref,
    rowt_ref,
    touched_ref,
    accum_ref,
    table_ref,
    wgrad_ref,
    bgrad_ref,
    dense_out_ref,
    accum_out_ref,
    table_out_ref,
):
    step = pl.program_id(0)
    count, width = rowt_ref.shape
    for c in range(wsum_ref.shape[0]):
        wgrad_ref[:, c * 128 : (c + 1) * 128] = wsum_ref[c].astype(F32) * scale
    dense_out_ref[...] = dense_ref[...]
    bgrad_ref[...] = bsum_ref[...] * scale

    source = jnp.concatenate([rowt_ref[...], jnp.ones((count, 128), BF16)], axis=1)
    blocks = table_ref.shape[0] // 128
    for i in range(blocks):
        block = step * blocks + i
        row_ids = block * 128 + lax.broadcasted_iota(jnp.int32, (128, count), 0)
        select = jnp.where(row_ids == touched_ref[...], 1.0, 0.0).astype(BF16)
        spread = jnp.dot(select, source, preferred_element_type=F32)
        grads = spread[:, :width]
        flipped = jnp.transpose(grads)
        square = jnp.sum(flipped * flipped, axis=0, keepdims=True)
        new_accum = accum_ref[pl.ds(block, 1), :] + square / width
        accum_out_ref[pl.ds(block, 1), :] = new_accum
        rate = jnp.transpose(jnp.broadcast_to(learn_rate / jnp.sqrt(new_accum), (width, 128)))
        r = pl.ds(i * 128, 128)
        rows = table_ref[r, :]
        table_out_ref[r, :] = jnp.where(
            spread[:, width:] > 0.5, keep_rate * rows - grads * rate, rows
        )


def update_call(scale, wsum, bsum, dense, rowt, touched, accum, table):
    pieces, d, _ = wsum.shape
    tok, width = dense.shape
    count = rowt.shape[0]
    shard_rows = table.shape[0]
    steps = 8

    def whole(shape):
        return pl.BlockSpec(shape, lambda i: (0,) * len(shape))

    return pl.pallas_call(
        functools.partial(update_kernel, scale),
        grid=(steps,),
        in_specs=[
            pl.BlockSpec((pieces, d // steps, 128), lambda i: (0, i, 0)),
            whole(bsum.shape),
            pl.BlockSpec((tok // steps, width), lambda i: (i, 0)),
            whole((count, width)),
            whole((1, count)),
            whole(accum.shape),
            pl.BlockSpec((shard_rows // steps, width), lambda i: (i, 0)),
        ],
        out_specs=(
            pl.BlockSpec((d // steps, d), lambda i: (i, 0)),
            whole(bsum.shape),
            pl.BlockSpec((tok // steps, width), lambda i: (i, 0)),
            whole(accum.shape),
            pl.BlockSpec((shard_rows // steps, width), lambda i: (i, 0)),
        ),
        out_shape=(
            jax.ShapeDtypeStruct((d, d), F32),
            jax.ShapeDtypeStruct(bsum.shape, F32),
            jax.ShapeDtypeStruct((tok, width), BF16),
            jax.ShapeDtypeStruct(accum.shape, F32),
            jax.ShapeDtypeStruct(table.shape, F32),
        ),
        compiler_params=pltpu.CompilerParams(vmem_limit_bytes=60 * 1024 * 1024),
    )(wsum, bsum, dense, rowt, touched, accum, table)


def per_device(
    n_rep,
    n_shard,
    features,
    cotangent,
    cross_weight,
    cross_bias,
    emb_table,
    row_accum,
    send_bags,
    slot_counts,
    recv_rows,
    touched_rows,
):
    tok = features.shape[0]
    width = emb_table.shape[1]
    scale = 1.0 / math.sqrt(tok * n_rep * n_shard)
    weight_sum, bias_sum, dense, rows = step_call(
        n_rep,
        n_shard,
        features,
        cotangent,
        cross_weight,
        cross_bias[None, :],
        send_bags[0],
        slot_counts,
        recv_rows[0],
        touched_rows,
        width,
    )
    weight_grad, bias_grad, dense_grad, new_accum, new_table = update_call(
        scale, weight_sum, bias_sum, dense, rows, touched_rows, row_accum.reshape(-1, 128), emb_table
    )
    return (weight_grad, bias_grad.reshape(-1), dense_grad, new_table, new_accum.reshape(-1))


def solution(mesh):
    in_specs = (
        P(("rep", "shard"), None),
        P(("rep", "shard"), None),
        P(),
        P(),
        P("shard", None),
        P("shard"),
        P(("rep", "shard"), None, None),
        P(("rep", "shard"), None),
        P(("rep", "shard"), None, None),
        P("shard", None),
    )
    out_specs = (P(), P(), P(("rep", "shard"), None), P("shard", None), P("shard"))
    return jax.shard_map(
        functools.partial(per_device, mesh.shape["rep"], mesh.shape["shard"]),
        mesh=mesh,
        in_specs=in_specs,
        out_specs=out_specs,
        check_vma=False,
    )
```

```python
import functools
import math

import jax
import jax.numpy as jnp
from jax import lax
from jax.experimental import pallas as pl
from jax.experimental.pallas import tpu as pltpu
from jax.sharding import PartitionSpec as P

learn_rate = 0.5
keep_rate = 0.9
MESH = pl.DeviceIdType.MESH
F32 = jnp.float32
BF16 = jnp.bfloat16


def step_kernel(
    n_rep,
    n_shard,
    feat_ref,
    cot_ref,
    w_hbm,
    cbias_ref,
    bags_ref,
    counts_ref,
    rows_ref,
    touched_ref,
    wsum_hbm,
    bsum_ref,
    dense_ref,
    rowt_ref,
    w_ref,
    wsum_ref,
    gated,
    ig,
    feat_t,
    wown,
    wsend,
    wpair,
    p1buf,
    p2buf,
    p3buf,
    bbuf1,
    bbuf2,
    bbuf3,
    outgoing,
    incoming,
    touched_col,
    rowacc,
    rowsend,
    rowbuf,
    p1_sem,
    p2_sem,
    p3_sem,
    b1_sem,
    b2_sem,
    b3_sem,
    a2a_sem,
    rrs_sem,
    rag_sem,
    agz_sem,
    agr_sem,
    agc_sem,
    w_sem,
    out_sem,
):
    nz = n_shard // 2
    rep = lax.axis_index("rep")
    shard = lax.axis_index("shard")
    core = lax.rem(shard, 2)
    zi = shard // 2
    partner = zi * 2 + (1 - core)
    tok, d = feat_ref.shape
    width = dense_ref.shape[1]
    feats = d // width - 1
    half = d // 2
    parts = half // 128
    rblk = d // n_rep
    zblk = rblk // nz
    touched_count = rowt_ref.shape[0]
    tblk = touched_count // n_rep
    slots = bags_ref.shape[1]
    inverse = (1 << 16) // feats + 1
    assert tok * feats * (inverse * feats - (1 << 16)) < 1 << 16

    def rep_peer(o):
        return lax.rem(rep + o, n_rep)

    def rep_from(o):
        return lax.rem(rep + n_rep - o, n_rep)

    def z_peer(o):
        return lax.rem(zi + o, nz)

    def z_from(o):
        return lax.rem(zi + nz - o, nz)

    def shard_peer(o):
        return lax.rem(shard + o, n_shard)

    def shard_from(o):
        return lax.rem(shard + n_shard - o, n_shard)

    def remote(src, dst, sems, index, target):
        return pltpu.make_async_remote_copy(
            src_ref=src,
            dst_ref=dst,
            send_sem=sems.at[0, index],
            recv_sem=sems.at[1, index],
            device_id=target,
            device_id_type=MESH,
        )

    def rep_rows(q):
        return pl.ds(pl.multiple_of(q * rblk, rblk), rblk)

    def z_rows(z):
        return pl.ds(pl.multiple_of(z * zblk, zblk), zblk)

    w_copy = pltpu.make_async_copy(w_hbm, w_ref, w_sem.at[0])
    w_copy.start()
    barrier = pltpu.get_barrier_semaphore()
    for o in range(1, n_shard):
        pl.semaphore_signal(
            barrier, inc=1, device_id={"shard": shard_peer(o)}, device_id_type=MESH
        )
    for o in range(1, n_rep):
        pl.semaphore_signal(barrier, inc=1, device_id={"rep": rep_peer(o)}, device_id_type=MESH)

    @pl.loop(0, tok // 128)
    def _(i):
        r = pl.ds(pl.multiple_of(i * 128, 128), 128)
        gated[r, :] = (cot_ref[r, :].astype(F32) * feat_ref[r, :].astype(F32)).astype(BF16)

    @pl.loop(0, d // 256)
    def _(i):
        r = pl.ds(pl.multiple_of(i * 256, 256), 256)
        feat_t[r, :] = jnp.transpose(feat_ref[:, r])

    def weight_pair(col_half, j, out, out_type):
        cols = pl.ds(pl.multiple_of(col_half * half + j * 256, 256), 256)

        @pl.loop(0, d // 256)
        def _(i):
            r = pl.ds(pl.multiple_of(i * 256, 256), 256)
            terms = jnp.dot(feat_t[r, :], gated[:, cols], preferred_element_type=F32)
            out[2 * j, r, :] = terms[:, :128].astype(out_type)
            out[2 * j + 1, r, :] = terms[:, 128:].astype(out_type)

    def p1(k):
        return remote(wsend.at[k], p1buf.at[k], p1_sem, k, {"shard": partner})

    for j in range(parts // 2):
        weight_pair(1 - core, j, wsend, BF16)
        if j == 0:
            pl.semaphore_wait(barrier, n_shard - 1 + n_rep - 1)
        p1(2 * j).start()
        p1(2 * j + 1).start()

    def p2(k, o):
        target = rep_peer(o)
        return remote(
            wpair.at[k, rep_rows(target), :],
            p2buf.at[k, o],
            p2_sem,
            k * n_rep + o,
            {"rep": target},
        )

    for j in range(parts // 2):
        weight_pair(core, j, wown, F32)
        for k in (2 * j, 2 * j + 1):
            p1(k).wait_recv()

            @pl.loop(0, n_rep)
            def _(i):
                r = rep_rows(i)
                wpair[k, r, :] = (wown[k, r, :] + p1buf[k, r, :].astype(F32)).astype(BF16)

            for o in range(1, n_rep):
                p2(k, o).start()

    bias_row = jnp.sum(gated[...].astype(F32), axis=0, keepdims=True)
    for j in range(d // 128):
        bbuf1[0, pl.ds(j, 1), :] = bias_row[:, j * 128 : (j + 1) * 128]
    b1 = remote(bbuf1.at[0], bbuf1.at[1], b1_sem, 0, {"shard": partner})
    b1.start()

    w_copy.wait()

    @pl.loop(0, d // 256)
    def _(i):
        c = pl.ds(pl.multiple_of(i * 256, 256), 256)
        linear = jnp.dot(feat_ref[...], w_ref[:, c], preferred_element_type=F32) + cbias_ref[:, c]
        back = lax.dot_general(
            gated[...], w_ref[c, :], (((1,), (1,)), ((), ())), preferred_element_type=F32
        )
        cot = cot_ref[:, c].astype(F32)
        ig[:, c] = (cot * linear + back + cot).astype(BF16)

    b1.wait_recv()
    bbuf2[rep] = bbuf1[0] + bbuf1[1]

    def b2(o, slot):
        return remote(bbuf2.at[slot], bbuf2.at[slot], b2_sem, o, {"rep": rep_peer(o)})

    for o in range(1, n_rep):
        b2(o, rep).start()

    def gather(dest):
        bags = bags_ref[pl.ds(dest, 1), :]
        place = lax.broadcasted_iota(jnp.int32, (1, slots), 1)
        sample = jnp.right_shift(bags * inverse, 16)
        code = jnp.where(place < counts_ref[0, dest], sample * 8 + (bags - sample * feats), -8)
        code = jnp.transpose(jnp.broadcast_to(code, (128, slots)))
        sample = jnp.right_shift(code, 3)
        feature = jnp.bitwise_and(code, 7)
        lane = lax.broadcasted_iota(jnp.int32, (slots, 128), 1)
        select = jnp.concatenate(
            [jnp.where(sample == lane + k * 128, 1.0, 0.0) for k in range(tok // 128)], axis=1
        ).astype(BF16)
        wide = jnp.dot(select, ig[:, width:], preferred_element_type=F32)
        picked = jnp.zeros((slots, width), F32)
        for f in range(feats):
            picked = jnp.where(feature == f, wide[:, f * width : (f + 1) * width], picked)
        return picked.astype(BF16)

    def a2a(o):
        dest = shard_peer(o)
        return remote(outgoing.at[dest], incoming.at[shard], a2a_sem, o, {"shard": dest})

    def a2a_in(o):
        src = shard_from(o)
        return remote(outgoing.at[src], incoming.at[src], a2a_sem, o, {"shard": src})

    def send_slots(low, high):
        @pl.loop(low, high)
        def _(o):
            outgoing[shard_peer(o)] = gather(shard_peer(o))
            a2a(o).start()

    def p3(k, o):
        target = z_peer(o)
        return remote(
            p2buf.at[k, 0, z_rows(target), :],
            p3buf.at[k, o],
            p3_sem,
            k * nz + o,
            {"shard": target * 2 + core},
        )

    def agz(k, o, z):
        place = wsum_ref.at[
            core * parts + k, pl.ds(pl.multiple_of(rep * rblk + z * zblk, zblk), zblk), :
        ]
        return remote(place, place, agz_sem, k * nz + o, {"shard": z_peer(o) * 2 + core})

    def agr(k, o, q):
        place = wsum_ref.at[core * parts + k, rep_rows(q), :]
        return remote(place, place, agr_sem, k * n_rep + o, {"rep": rep_peer(o)})

    def agc(k, o, q, side):
        place = wsum_ref.at[side * parts + k, rep_rows(q), :]
        return remote(place, place, agc_sem, k * n_rep + o, {"shard": partner})

    cuts = (1, n_shard // 2 - 1, n_shard - 2, n_shard)
    for t in range(parts + 2):
        if t < parts:
            k = t
            for o in range(1, n_rep):
                p2(k, o).wait_recv()
            total = wpair[k, rep_rows(rep), :].astype(F32)
            for o in range(1, n_rep):
                total = total + p2buf[k, o].astype(F32)
            p2buf[k, 0] = total.astype(BF16)
            for o in range(1, nz):
                p3(k, o).start()
            if t < 3:
                send_slots(cuts[t], cuts[t + 1])
        if 1 <= t <= parts:
            k = t - 1
            for o in range(1, nz):
                p3(k, o).wait_recv()
            block = p2buf[k, 0, z_rows(zi), :].astype(F32)
            for o in range(1, nz):
                block = block + p3buf[k, o].astype(F32)
            mine = pl.ds(pl.multiple_of(rep * rblk + zi * zblk, zblk), zblk)
            wsum_ref[core * parts + k, mine, :] = block.astype(BF16)
            for o in range(1, nz):
                agz(k, o, zi).start()
        if 2 <= t:
            k = t - 2
            for o in range(1, nz):
                agz(k, o, z_from(o)).wait_recv()
            for o in range(1, n_rep):
                agr(k, o, rep).start()
            agc(k, 0, rep, core).start()

    incoming[shard] = gather(shard)
    dense_ref[...] = ig[:, :width]
    touched_col[...] = jnp.transpose(
        jnp.broadcast_to(touched_ref[...], (128, touched_count))
    )
    for o in range(1, n_rep):
        b2(o, rep_from(o)).wait_recv()
    bias_rep = bbuf2[0]
    for q in range(1, n_rep):
        bias_rep = bias_rep + bbuf2[q]
    bbuf3[zi] = bias_rep

    def b3(o, slot):
        return remote(
            bbuf3.at[slot], bbuf3.at[slot], b3_sem, o, {"shard": z_peer(o) * 2 + core}
        )

    for o in range(1, nz):
        b3(o, zi).start()

    def add_source(src):
        rows = rows_ref[pl.ds(src, 1), :]
        select = jnp.concatenate(
            [
                jnp.where(touched_col[...] == rows[:, k * 128 : (k + 1) * 128], 1.0, 0.0)
                for k in range(slots // 128)
            ],
            axis=1,
        ).astype(BF16)
        return jnp.dot(select, incoming[src], preferred_element_type=F32)

    rowacc[...] = add_source(shard)

    @pl.loop(1, n_shard)
    def _(o):
        a2a_in(o).wait_recv()
        rowacc[...] += add_source(shard_from(o))

    rowsend[...] = rowacc[...].astype(BF16)

    def rrs(o):
        target = rep_peer(o)
        r = pl.ds(pl.multiple_of(target * tblk, tblk), tblk)
        return remote(rowsend.at[r, :], rowbuf.at[o], rrs_sem, o, {"rep": target})

    for o in range(1, n_rep):
        rrs(o).start()

    def write_out(side, k):
        piece = side * parts + k
        return pltpu.make_async_copy(wsum_ref.at[piece], wsum_hbm.at[piece], out_sem.at[piece])

    for k in range(parts // 2):
        for o in range(1, n_rep):
            agr(k, o, rep_from(o)).wait_recv()
            agc(k, o, rep_from(o), core).start()
        write_out(core, k).start()

    for o in range(1, n_rep):
        rrs(o).wait_recv()
    own = pl.ds(pl.multiple_of(rep * tblk, tblk), tblk)
    row_total = rowacc[own, :]
    for o in range(1, n_rep):
        row_total = row_total + rowbuf[o].astype(F32)
    rowt_ref[own, :] = row_total.astype(BF16)

    def rag(o, q):
        place = rowt_ref.at[pl.ds(pl.multiple_of(q * tblk, tblk), tblk), :]
        return remote(place, place, rag_sem, o, {"rep": rep_peer(o)})

    for o in range(1, n_rep):
        rag(o, rep).start()

    for o in range(1, nz):
        b3(o, z_from(o)).wait_recv()
    bias_all = bbuf3[0]
    for z in range(1, nz):
        bias_all = bias_all + bbuf3[z]
    bsum_ref[...] = bias_all

    for k in range(parts // 2, parts):
        for o in range(1, n_rep):
            agr(k, o, rep_from(o)).wait_recv()
            agc(k, o, rep_from(o), core).start()
        write_out(core, k).start()
    for o in range(1, n_rep):
        rag(o, rep_from(o)).wait_recv()
    for k in range(parts):
        for o in range(n_rep):
            agc(k, o, rep_from(o), 1 - core).wait_recv()
        write_out(1 - core, k).start()

    b1.wait_send()
    for o in range(1, n_rep):
        b2(o, rep).wait_send()
        rrs(o).wait_send()
        rag(o, rep).wait_send()
    for o in range(1, nz):
        b3(o, zi).wait_send()
    for k in range(parts):
        p1(k).wait_send()
        for o in range(1, n_rep):
            p2(k, o).wait_send()
            agr(k, o, rep).wait_send()
        for o in range(1, nz):
            p3(k, o).wait_send()
            agz(k, o, zi).wait_send()
        for o in range(n_rep):
            agc(k, o, rep_from(o), core).wait_send()
        write_out(core, k).wait()
        write_out(1 - core, k).wait()

    @pl.loop(1, n_shard)
    def _(o):
        a2a(o).wait_send()


def step_call(n_rep, n_shard, feats, cot, weight, cbias, bags, counts, rows, touched, width):
    tok, d = feats.shape
    nz = n_shard // 2
    slots = bags.shape[1]
    count = touched.shape[1]
    half = d // 2
    parts = half // 128
    rblk = d // n_rep
    zblk = rblk // nz
    tblk = count // n_rep
    vmem = pl.BlockSpec(memory_space=pltpu.VMEM)
    smem = pl.BlockSpec(memory_space=pltpu.SMEM)
    hbm = pl.BlockSpec(memory_space=pl.ANY)

    def sems(n):
        return pltpu.SemaphoreType.DMA((2, n))

    return pl.pallas_call(
        functools.partial(step_kernel, n_rep, n_shard),
        out_shape=(
            jax.ShapeDtypeStruct((2 * parts, d, 128), BF16),
            jax.ShapeDtypeStruct((d // 128, 128), F32),
            jax.ShapeDtypeStruct((tok, width), BF16),
            jax.ShapeDtypeStruct((count, width), BF16),
        ),
        in_specs=[vmem, vmem, hbm, vmem, vmem, smem, vmem, vmem],
        out_specs=(hbm, vmem, vmem, vmem),
        scratch_shapes=[
            pltpu.VMEM((d, d), BF16),
            pltpu.VMEM((2 * parts, d, 128), BF16),
            pltpu.VMEM((tok, d), BF16),
            pltpu.VMEM((tok, d), BF16),
            pltpu.VMEM((d, tok), BF16),
            pltpu.VMEM((parts, d, 128), F32),
            pltpu.VMEM((parts, d, 128), BF16),
            pltpu.VMEM((parts, d, 128), BF16),
            pltpu.VMEM((parts, d, 128), BF16),
            pltpu.VMEM((parts, n_rep, rblk, 128), BF16),
            pltpu.VMEM((parts, nz, zblk, 128), BF16),
            pltpu.VMEM((2, d // 128, 128), F32),
            pltpu.VMEM((n_rep, d // 128, 128), F32),
            pltpu.VMEM((nz, d // 128, 128), F32),
            pltpu.VMEM((n_shard, slots, width), BF16),
            pltpu.VMEM((n_shard, slots, width), BF16),
            pltpu.VMEM((count, 128), jnp.int32),
            pltpu.VMEM((count, width), F32),
            pltpu.VMEM((count, width), BF16),
            pltpu.VMEM((n_rep, tblk, width), BF16),
            sems(parts),
            sems(parts * n_rep),
            sems(parts * nz),
            sems(1),
            sems(n_rep),
            sems(nz),
            sems(n_shard),
            sems(n_rep),
            sems(n_rep),
            sems(parts * nz),
            sems(parts * n_rep),
            sems(parts * n_rep),
            pltpu.SemaphoreType.DMA((1,)),
            pltpu.SemaphoreType.DMA((2 * parts,)),
        ],
        compiler_params=pltpu.CompilerParams(
            collective_id=0, has_side_effects=True, vmem_limit_bytes=60 * 1024 * 1024
        ),
    )(feats, cot, weight, cbias, bags, counts, rows, touched)


def update_kernel(
    scale,
    wsum_ref,
    bsum_ref,
    dense_ref,
    rowt_ref,
    touched_ref,
    accum_ref,
    table_ref,
    wgrad_ref,
    bgrad_ref,
    dense_out_ref,
    accum_out_ref,
    table_out_ref,
):
    step = pl.program_id(0)
    count, width = rowt_ref.shape
    for c in range(wsum_ref.shape[0]):
        wgrad_ref[:, c * 128 : (c + 1) * 128] = wsum_ref[c].astype(F32) * scale
    dense_out_ref[...] = dense_ref[...]
    bgrad_ref[...] = bsum_ref[...] * scale

    source = jnp.concatenate([rowt_ref[...], jnp.ones((count, 128), BF16)], axis=1)
    rows_here = table_ref.shape[0]
    blocks = rows_here // 128
    row_ids = step * rows_here + lax.broadcasted_iota(jnp.int32, (rows_here, count), 0)
    select = jnp.where(row_ids == touched_ref[...], 1.0, 0.0).astype(BF16)
    spread = jnp.dot(select, source, preferred_element_type=F32)
    grads = spread[:, :width]
    flipped = jnp.transpose(grads)
    square = jnp.sum(flipped * flipped, axis=0, keepdims=True) / width
    rates = []
    for i in range(blocks):
        place = pl.ds(step * blocks + i, 1)
        new_accum = accum_ref[place, :] + square[:, i * 128 : (i + 1) * 128]
        accum_out_ref[place, :] = new_accum
        rates.append(learn_rate / jnp.sqrt(new_accum))
    rate = jnp.concatenate(rates, axis=1)
    rate = jnp.transpose(jnp.broadcast_to(rate, (width, rows_here)))
    rows = table_ref[...]
    table_out_ref[...] = jnp.where(spread[:, width:] > 0.5, keep_rate * rows - grads * rate, rows)


def update_call(scale, wsum, bsum, dense, rowt, touched, accum, table):
    pieces, d, _ = wsum.shape
    tok, width = dense.shape
    count = rowt.shape[0]
    shard_rows = table.shape[0]
    steps = 8

    def whole(shape):
        return pl.BlockSpec(shape, lambda i: (0,) * len(shape))

    return pl.pallas_call(
        functools.partial(update_kernel, scale),
        grid=(steps,),
        in_specs=[
            pl.BlockSpec((pieces, d // steps, 128), lambda i: (0, i, 0)),
            whole(bsum.shape),
            pl.BlockSpec((tok // steps, width), lambda i: (i, 0)),
            whole((count, width)),
            whole((1, count)),
            whole(accum.shape),
            pl.BlockSpec((shard_rows // steps, width), lambda i: (i, 0)),
        ],
        out_specs=(
            pl.BlockSpec((d // steps, d), lambda i: (i, 0)),
            whole(bsum.shape),
            pl.BlockSpec((tok // steps, width), lambda i: (i, 0)),
            whole(accum.shape),
            pl.BlockSpec((shard_rows // steps, width), lambda i: (i, 0)),
        ),
        out_shape=(
            jax.ShapeDtypeStruct((d, d), F32),
            jax.ShapeDtypeStruct(bsum.shape, F32),
            jax.ShapeDtypeStruct((tok, width), BF16),
            jax.ShapeDtypeStruct(accum.shape, F32),
            jax.ShapeDtypeStruct(table.shape, F32),
        ),
        compiler_params=pltpu.CompilerParams(vmem_limit_bytes=60 * 1024 * 1024),
    )(wsum, bsum, dense, rowt, touched, accum, table)


def per_device(
    n_rep,
    n_shard,
    features,
    cotangent,
    cross_weight,
    cross_bias,
    emb_table,
    row_accum,
    send_bags,
    slot_counts,
    recv_rows,
    touched_rows,
):
    tok = features.shape[0]
    width = emb_table.shape[1]
    scale = 1.0 / math.sqrt(tok * n_rep * n_shard)
    weight_sum, bias_sum, dense, rows = step_call(
        n_rep,
        n_shard,
        features,
        cotangent,
        cross_weight,
        cross_bias[None, :],
        send_bags[0],
        slot_counts,
        recv_rows[0],
        touched_rows,
        width,
    )
    weight_grad, bias_grad, dense_grad, new_accum, new_table = update_call(
        scale, weight_sum, bias_sum, dense, rows, touched_rows, row_accum.reshape(-1, 128), emb_table
    )
    return (weight_grad, bias_grad.reshape(-1), dense_grad, new_table, new_accum.reshape(-1))


def solution(mesh):
    in_specs = (
        P(("rep", "shard"), None),
        P(("rep", "shard"), None),
        P(),
        P(),
        P("shard", None),
        P("shard"),
        P(("rep", "shard"), None, None),
        P(("rep", "shard"), None),
        P(("rep", "shard"), None, None),
        P("shard", None),
    )
    out_specs = (P(), P(), P(("rep", "shard"), None), P("shard", None), P("shard"))
    return jax.shard_map(
        functools.partial(per_device, mesh.shape["rep"], mesh.shape["shard"]),
        mesh=mesh,
        in_specs=in_specs,
        out_specs=out_specs,
        check_vma=False,
    )
```

```python
import functools
import math

import jax
import jax.numpy as jnp
from jax import lax
from jax.experimental import pallas as pl
from jax.experimental.pallas import tpu as pltpu
from jax.sharding import PartitionSpec as P

learn_rate = 0.5
keep_rate = 0.9
MESH = pl.DeviceIdType.MESH
F32 = jnp.float32
BF16 = jnp.bfloat16


def step_kernel(
    n_rep,
    n_shard,
    feat_ref,
    cot_ref,
    w_hbm,
    cbias_ref,
    bags_ref,
    counts_ref,
    rows_ref,
    touched_ref,
    wsum_hbm,
    bsum_ref,
    dense_ref,
    rowt_ref,
    w_ref,
    wsum_ref,
    gated,
    ig,
    feat_t,
    wown,
    wsend,
    wpair,
    p1buf,
    p2buf,
    p3buf,
    bbuf1,
    bbuf2,
    bbuf3,
    outgoing,
    incoming,
    touched_col,
    rowacc,
    rowsend,
    rowbuf,
    p1_sem,
    p2_sem,
    p3_sem,
    b1_sem,
    b2_sem,
    b3_sem,
    a2a_sem,
    rrs_sem,
    rag_sem,
    agz_sem,
    agr_sem,
    agc_sem,
    w_sem,
    out_sem,
):
    nz = n_shard // 2
    rep = lax.axis_index("rep")
    shard = lax.axis_index("shard")
    core = lax.rem(shard, 2)
    zi = shard // 2
    partner = zi * 2 + (1 - core)
    tok, d = feat_ref.shape
    width = dense_ref.shape[1]
    feats = d // width - 1
    half = d // 2
    parts = half // 128
    rblk = d // n_rep
    zblk = rblk // nz
    touched_count = rowt_ref.shape[0]
    tblk = touched_count // n_rep
    slots = bags_ref.shape[1]
    inverse = (1 << 16) // feats + 1
    assert n_rep == 4
    assert tok * feats * (inverse * feats - (1 << 16)) < 1 << 16

    def rep_peer(o):
        return lax.rem(rep + o, n_rep)

    def rep_from(o):
        return lax.rem(rep + n_rep - o, n_rep)

    def z_peer(o):
        return lax.rem(zi + o, nz)

    def z_from(o):
        return lax.rem(zi + nz - o, nz)

    def shard_peer(o):
        return lax.rem(shard + o, n_shard)

    def shard_from(o):
        return lax.rem(shard + n_shard - o, n_shard)

    def remote(src, dst, sems, index, target):
        return pltpu.make_async_remote_copy(
            src_ref=src,
            dst_ref=dst,
            send_sem=sems.at[0, index],
            recv_sem=sems.at[1, index],
            device_id=target,
            device_id_type=MESH,
        )

    def rep_rows(q):
        return pl.ds(pl.multiple_of(q * rblk, rblk), rblk)

    def z_rows(z):
        return pl.ds(pl.multiple_of(z * zblk, zblk), zblk)

    w_copy = pltpu.make_async_copy(w_hbm, w_ref, w_sem.at[0])
    w_copy.start()
    barrier = pltpu.get_barrier_semaphore()
    for o in range(1, n_shard):
        pl.semaphore_signal(
            barrier, inc=1, device_id={"shard": shard_peer(o)}, device_id_type=MESH
        )
    for o in range(1, n_rep):
        pl.semaphore_signal(barrier, inc=1, device_id={"rep": rep_peer(o)}, device_id_type=MESH)

    @pl.loop(0, tok // 128)
    def _(i):
        r = pl.ds(pl.multiple_of(i * 128, 128), 128)
        gated[r, :] = (cot_ref[r, :].astype(F32) * feat_ref[r, :].astype(F32)).astype(BF16)

    @pl.loop(0, d // 256)
    def _(i):
        r = pl.ds(pl.multiple_of(i * 256, 256), 256)
        feat_t[r, :] = jnp.transpose(feat_ref[:, r])

    def weight_pair(col_half, j, out, out_type):
        cols = pl.ds(pl.multiple_of(col_half * half + j * 256, 256), 256)

        @pl.loop(0, d // 256)
        def _(i):
            r = pl.ds(pl.multiple_of(i * 256, 256), 256)
            terms = jnp.dot(feat_t[r, :], gated[:, cols], preferred_element_type=F32)
            out[2 * j, r, :] = terms[:, :128].astype(out_type)
            out[2 * j + 1, r, :] = terms[:, 128:].astype(out_type)

    def p1(k):
        return remote(wsend.at[k], p1buf.at[k], p1_sem, k, {"shard": partner})

    for j in range(parts // 2):
        weight_pair(1 - core, j, wsend, BF16)
        if j == 0:
            pl.semaphore_wait(barrier, n_shard - 1 + n_rep - 1)
        p1(2 * j).start()
        p1(2 * j + 1).start()

    def p2(k, o):
        target = rep_peer(o)
        return remote(
            wpair.at[k, rep_rows(target), :],
            p2buf.at[k, o],
            p2_sem,
            k * n_rep + o,
            {"rep": target},
        )

    for j in range(parts // 2):
        weight_pair(core, j, wown, F32)
        for k in (2 * j, 2 * j + 1):
            p1(k).wait_recv()

            @pl.loop(0, n_rep)
            def _(i):
                r = rep_rows(i)
                wpair[k, r, :] = (wown[k, r, :] + p1buf[k, r, :].astype(F32)).astype(BF16)

            for o in range(1, n_rep):
                p2(k, o).start()

    bias_row = jnp.sum(gated[...].astype(F32), axis=0, keepdims=True)
    for j in range(d // 128):
        bbuf1[0, pl.ds(j, 1), :] = bias_row[:, j * 128 : (j + 1) * 128]
    b1 = remote(bbuf1.at[0], bbuf1.at[1], b1_sem, 0, {"shard": partner})
    b1.start()

    w_copy.wait()

    @pl.loop(0, d // 256)
    def _(i):
        c = pl.ds(pl.multiple_of(i * 256, 256), 256)
        linear = jnp.dot(feat_ref[...], w_ref[:, c], preferred_element_type=F32) + cbias_ref[:, c]
        back = lax.dot_general(
            gated[...], w_ref[c, :], (((1,), (1,)), ((), ())), preferred_element_type=F32
        )
        cot = cot_ref[:, c].astype(F32)
        ig[:, c] = (cot * linear + back + cot).astype(BF16)

    b1.wait_recv()
    bbuf2[rep] = bbuf1[0] + bbuf1[1]

    def b2(o, slot):
        return remote(bbuf2.at[slot], bbuf2.at[slot], b2_sem, o, {"rep": rep_peer(o)})

    for o in range(1, n_rep):
        b2(o, rep).start()

    def gather(dest):
        bags = bags_ref[pl.ds(dest, 1), :]
        place = lax.broadcasted_iota(jnp.int32, (1, slots), 1)
        sample = jnp.right_shift(bags * inverse, 16)
        code = jnp.where(place < counts_ref[0, dest], sample * 8 + (bags - sample * feats), -8)
        code = jnp.transpose(jnp.broadcast_to(code, (128, slots)))
        sample = jnp.right_shift(code, 3)
        feature = jnp.bitwise_and(code, 7)
        lane = lax.broadcasted_iota(jnp.int32, (slots, 128), 1)
        select = jnp.concatenate(
            [jnp.where(sample == lane + k * 128, 1.0, 0.0) for k in range(tok // 128)], axis=1
        ).astype(BF16)
        wide = jnp.dot(select, ig[:, width:], preferred_element_type=F32)
        picked = jnp.zeros((slots, width), F32)
        for f in range(feats):
            picked = jnp.where(feature == f, wide[:, f * width : (f + 1) * width], picked)
        return picked.astype(BF16)

    def a2a(o):
        dest = shard_peer(o)
        return remote(outgoing.at[dest], incoming.at[shard], a2a_sem, o, {"shard": dest})

    def a2a_in(o):
        src = shard_from(o)
        return remote(outgoing.at[src], incoming.at[src], a2a_sem, o, {"shard": src})

    def send_slots(low, high):
        @pl.loop(low, high)
        def _(o):
            outgoing[shard_peer(o)] = gather(shard_peer(o))
            a2a(o).start()

    def p3(k, o):
        target = z_peer(o)
        return remote(
            p2buf.at[k, 0, z_rows(target), :],
            p3buf.at[k, o],
            p3_sem,
            k * nz + o,
            {"shard": target * 2 + core},
        )

    def agz(k, o, z):
        place = wsum_ref.at[
            core * parts + k, pl.ds(pl.multiple_of(rep * rblk + z * zblk, zblk), zblk), :
        ]
        return remote(place, place, agz_sem, k * nz + o, {"shard": z_peer(o) * 2 + core})

    def flip(mask):
        if mask == 1:
            return rep + 1 - 2 * lax.rem(rep, 2)
        return lax.rem(rep + 2, 4) if mask == 2 else 3 - rep

    def owner(k, o):
        return rep if o == 0 else flip((2 - k % 2, 1 + k % 2, 3)[o - 1])

    def agr(k, o, arriving=False):
        q = owner(k, o) if arriving else owner(k, 1 if o == 3 else 0)
        place = wsum_ref.at[core * parts + k, rep_rows(q), :]
        target = owner(k, 1 if o == 1 else 2)
        return remote(place, place, agr_sem, k * n_rep + o, {"rep": target})

    def agc(k, o, side):
        place = wsum_ref.at[side * parts + k, rep_rows(owner(k, o)), :]
        return remote(place, place, agc_sem, k * n_rep + o, {"shard": partner})

    def forward(k):
        agr(k, 1, True).wait_recv()
        agr(k, 3).start()
        agc(k, 1, core).start()

    def write_out(side, k):
        piece = side * parts + k
        return pltpu.make_async_copy(wsum_ref.at[piece], wsum_hbm.at[piece], out_sem.at[piece])

    def finish(k):
        for o in (2, 3):
            agr(k, o, True).wait_recv()
            agc(k, o, core).start()
        write_out(core, k).start()

    cuts = (1, n_shard // 2 - 1, n_shard - 2, n_shard)
    for t in range(parts + 2):
        if t < parts:
            k = t
            for o in range(1, n_rep):
                p2(k, o).wait_recv()
            total = wpair[k, rep_rows(rep), :].astype(F32)
            for o in range(1, n_rep):
                total = total + p2buf[k, o].astype(F32)
            p2buf[k, 0] = total.astype(BF16)
            for o in range(1, nz):
                p3(k, o).start()
            if t < 3:
                send_slots(cuts[t], cuts[t + 1])
        if 1 <= t <= parts:
            k = t - 1
            for o in range(1, nz):
                p3(k, o).wait_recv()
            block = p2buf[k, 0, z_rows(zi), :].astype(F32)
            for o in range(1, nz):
                block = block + p3buf[k, o].astype(F32)
            mine = pl.ds(pl.multiple_of(rep * rblk + zi * zblk, zblk), zblk)
            wsum_ref[core * parts + k, mine, :] = block.astype(BF16)
            for o in range(1, nz):
                agz(k, o, zi).start()
        if 2 <= t:
            k = t - 2
            for o in range(1, nz):
                agz(k, o, z_from(o)).wait_recv()
            for o in (1, 2):
                agr(k, o).start()
            agc(k, 0, core).start()

    for k in range(parts - 1):
        forward(k)

    incoming[shard] = gather(shard)
    dense_ref[...] = ig[:, :width]
    touched_col[...] = jnp.transpose(
        jnp.broadcast_to(touched_ref[...], (128, touched_count))
    )
    for o in range(1, n_rep):
        b2(o, rep_from(o)).wait_recv()
    bias_rep = bbuf2[0]
    for q in range(1, n_rep):
        bias_rep = bias_rep + bbuf2[q]
    bbuf3[zi] = bias_rep

    def b3(o, slot):
        return remote(
            bbuf3.at[slot], bbuf3.at[slot], b3_sem, o, {"shard": z_peer(o) * 2 + core}
        )

    for o in range(1, nz):
        b3(o, zi).start()

    def add_source(src):
        rows = rows_ref[pl.ds(src, 1), :]
        select = jnp.concatenate(
            [
                jnp.where(touched_col[...] == rows[:, k * 128 : (k + 1) * 128], 1.0, 0.0)
                for k in range(slots // 128)
            ],
            axis=1,
        ).astype(BF16)
        return jnp.dot(select, incoming[src], preferred_element_type=F32)

    rowacc[...] = add_source(shard)

    @pl.loop(1, n_shard)
    def _(o):
        a2a_in(o).wait_recv()
        rowacc[...] += add_source(shard_from(o))

    rowsend[...] = rowacc[...].astype(BF16)

    def rrs(o):
        target = rep_peer(o)
        r = pl.ds(pl.multiple_of(target * tblk, tblk), tblk)
        return remote(rowsend.at[r, :], rowbuf.at[o], rrs_sem, o, {"rep": target})

    for o in range(1, n_rep):
        rrs(o).start()

    forward(parts - 1)
    for k in range(parts // 2):
        finish(k)

    for o in range(1, n_rep):
        rrs(o).wait_recv()
    own = pl.ds(pl.multiple_of(rep * tblk, tblk), tblk)
    row_total = rowacc[own, :]
    for o in range(1, n_rep):
        row_total = row_total + rowbuf[o].astype(F32)
    rowt_ref[own, :] = row_total.astype(BF16)

    def rag(o, q):
        place = rowt_ref.at[pl.ds(pl.multiple_of(q * tblk, tblk), tblk), :]
        return remote(place, place, rag_sem, o, {"rep": rep_peer(o)})

    for o in range(1, n_rep):
        rag(o, rep).start()

    for o in range(1, nz):
        b3(o, z_from(o)).wait_recv()
    bias_all = bbuf3[0]
    for z in range(1, nz):
        bias_all = bias_all + bbuf3[z]
    bsum_ref[...] = bias_all

    for k in range(parts // 2, parts):
        finish(k)
    for o in range(1, n_rep):
        rag(o, rep_from(o)).wait_recv()
    for k in range(parts):
        for o in range(n_rep):
            agc(k, o, 1 - core).wait_recv()
        write_out(1 - core, k).start()

    b1.wait_send()
    for o in range(1, n_rep):
        b2(o, rep).wait_send()
        rrs(o).wait_send()
        rag(o, rep).wait_send()
    for o in range(1, nz):
        b3(o, zi).wait_send()
    for k in range(parts):
        p1(k).wait_send()
        for o in range(1, n_rep):
            p2(k, o).wait_send()
            agr(k, o).wait_send()
        for o in range(1, nz):
            p3(k, o).wait_send()
            agz(k, o, zi).wait_send()
        for o in range(n_rep):
            agc(k, o, core).wait_send()
        write_out(core, k).wait()
        write_out(1 - core, k).wait()

    @pl.loop(1, n_shard)
    def _(o):
        a2a(o).wait_send()


def step_call(n_rep, n_shard, feats, cot, weight, cbias, bags, counts, rows, touched, width):
    tok, d = feats.shape
    nz = n_shard // 2
    slots = bags.shape[1]
    count = touched.shape[1]
    half = d // 2
    parts = half // 128
    rblk = d // n_rep
    zblk = rblk // nz
    tblk = count // n_rep
    vmem = pl.BlockSpec(memory_space=pltpu.VMEM)
    smem = pl.BlockSpec(memory_space=pltpu.SMEM)
    hbm = pl.BlockSpec(memory_space=pl.ANY)

    def sems(n):
        return pltpu.SemaphoreType.DMA((2, n))

    return pl.pallas_call(
        functools.partial(step_kernel, n_rep, n_shard),
        out_shape=(
            jax.ShapeDtypeStruct((2 * parts, d, 128), BF16),
            jax.ShapeDtypeStruct((d // 128, 128), F32),
            jax.ShapeDtypeStruct((tok, width), BF16),
            jax.ShapeDtypeStruct((count, width), BF16),
        ),
        in_specs=[vmem, vmem, hbm, vmem, vmem, smem, vmem, vmem],
        out_specs=(hbm, vmem, vmem, vmem),
        scratch_shapes=[
            pltpu.VMEM((d, d), BF16),
            pltpu.VMEM((2 * parts, d, 128), BF16),
            pltpu.VMEM((tok, d), BF16),
            pltpu.VMEM((tok, d), BF16),
            pltpu.VMEM((d, tok), BF16),
            pltpu.VMEM((parts, d, 128), F32),
            pltpu.VMEM((parts, d, 128), BF16),
            pltpu.VMEM((parts, d, 128), BF16),
            pltpu.VMEM((parts, d, 128), BF16),
            pltpu.VMEM((parts, n_rep, rblk, 128), BF16),
            pltpu.VMEM((parts, nz, zblk, 128), BF16),
            pltpu.VMEM((2, d // 128, 128), F32),
            pltpu.VMEM((n_rep, d // 128, 128), F32),
            pltpu.VMEM((nz, d // 128, 128), F32),
            pltpu.VMEM((n_shard, slots, width), BF16),
            pltpu.VMEM((n_shard, slots, width), BF16),
            pltpu.VMEM((count, 128), jnp.int32),
            pltpu.VMEM((count, width), F32),
            pltpu.VMEM((count, width), BF16),
            pltpu.VMEM((n_rep, tblk, width), BF16),
            sems(parts),
            sems(parts * n_rep),
            sems(parts * nz),
            sems(1),
            sems(n_rep),
            sems(nz),
            sems(n_shard),
            sems(n_rep),
            sems(n_rep),
            sems(parts * nz),
            sems(parts * n_rep),
            sems(parts * n_rep),
            pltpu.SemaphoreType.DMA((1,)),
            pltpu.SemaphoreType.DMA((2 * parts,)),
        ],
        compiler_params=pltpu.CompilerParams(
            collective_id=0, has_side_effects=True, vmem_limit_bytes=60 * 1024 * 1024
        ),
    )(feats, cot, weight, cbias, bags, counts, rows, touched)


def update_kernel(
    scale,
    wsum_ref,
    bsum_ref,
    dense_ref,
    rowt_ref,
    touched_ref,
    accum_ref,
    table_ref,
    wgrad_ref,
    bgrad_ref,
    dense_out_ref,
    accum_out_ref,
    table_out_ref,
):
    step = pl.program_id(0)
    count, width = rowt_ref.shape
    for c in range(wsum_ref.shape[0]):
        wgrad_ref[:, c * 128 : (c + 1) * 128] = wsum_ref[c].astype(F32) * scale
    dense_out_ref[...] = dense_ref[...]
    bgrad_ref[...] = bsum_ref[...] * scale

    source = jnp.concatenate([rowt_ref[...], jnp.ones((count, 128), BF16)], axis=1)
    rows_here = table_ref.shape[0]
    blocks = rows_here // 128
    row_ids = step * rows_here + lax.broadcasted_iota(jnp.int32, (rows_here, count), 0)
    select = jnp.where(row_ids == touched_ref[...], 1.0, 0.0).astype(BF16)
    spread = jnp.dot(select, source, preferred_element_type=F32)
    grads = spread[:, :width]
    flipped = jnp.transpose(grads)
    square = jnp.sum(flipped * flipped, axis=0, keepdims=True) / width
    rates = []
    for i in range(blocks):
        place = pl.ds(step * blocks + i, 1)
        new_accum = accum_ref[place, :] + square[:, i * 128 : (i + 1) * 128]
        accum_out_ref[place, :] = new_accum
        rates.append(learn_rate / jnp.sqrt(new_accum))
    rate = jnp.concatenate(rates, axis=1)
    rate = jnp.transpose(jnp.broadcast_to(rate, (width, rows_here)))
    rows = table_ref[...]
    table_out_ref[...] = jnp.where(spread[:, width:] > 0.5, keep_rate * rows - grads * rate, rows)


def update_call(scale, wsum, bsum, dense, rowt, touched, accum, table):
    pieces, d, _ = wsum.shape
    tok, width = dense.shape
    count = rowt.shape[0]
    shard_rows = table.shape[0]
    steps = 8

    def whole(shape):
        return pl.BlockSpec(shape, lambda i: (0,) * len(shape))

    return pl.pallas_call(
        functools.partial(update_kernel, scale),
        grid=(steps,),
        in_specs=[
            pl.BlockSpec((pieces, d // steps, 128), lambda i: (0, i, 0)),
            whole(bsum.shape),
            pl.BlockSpec((tok // steps, width), lambda i: (i, 0)),
            whole((count, width)),
            whole((1, count)),
            whole(accum.shape),
            pl.BlockSpec((shard_rows // steps, width), lambda i: (i, 0)),
        ],
        out_specs=(
            pl.BlockSpec((d // steps, d), lambda i: (i, 0)),
            whole(bsum.shape),
            pl.BlockSpec((tok // steps, width), lambda i: (i, 0)),
            whole(accum.shape),
            pl.BlockSpec((shard_rows // steps, width), lambda i: (i, 0)),
        ),
        out_shape=(
            jax.ShapeDtypeStruct((d, d), F32),
            jax.ShapeDtypeStruct(bsum.shape, F32),
            jax.ShapeDtypeStruct((tok, width), BF16),
            jax.ShapeDtypeStruct(accum.shape, F32),
            jax.ShapeDtypeStruct(table.shape, F32),
        ),
        compiler_params=pltpu.CompilerParams(vmem_limit_bytes=60 * 1024 * 1024),
    )(wsum, bsum, dense, rowt, touched, accum, table)


def per_device(
    n_rep,
    n_shard,
    features,
    cotangent,
    cross_weight,
    cross_bias,
    emb_table,
    row_accum,
    send_bags,
    slot_counts,
    recv_rows,
    touched_rows,
):
    tok = features.shape[0]
    width = emb_table.shape[1]
    scale = 1.0 / math.sqrt(tok * n_rep * n_shard)
    weight_sum, bias_sum, dense, rows = step_call(
        n_rep,
        n_shard,
        features,
        cotangent,
        cross_weight,
        cross_bias[None, :],
        send_bags[0],
        slot_counts,
        recv_rows[0],
        touched_rows,
        width,
    )
    weight_grad, bias_grad, dense_grad, new_accum, new_table = update_call(
        scale, weight_sum, bias_sum, dense, rows, touched_rows, row_accum.reshape(-1, 128), emb_table
    )
    return (weight_grad, bias_grad.reshape(-1), dense_grad, new_table, new_accum.reshape(-1))


def solution(mesh):
    in_specs = (
        P(("rep", "shard"), None),
        P(("rep", "shard"), None),
        P(),
        P(),
        P("shard", None),
        P("shard"),
        P(("rep", "shard"), None, None),
        P(("rep", "shard"), None),
        P(("rep", "shard"), None, None),
        P("shard", None),
    )
    out_specs = (P(), P(), P(("rep", "shard"), None), P("shard", None), P("shard"))
    return jax.shard_map(
        functools.partial(per_device, mesh.shape["rep"], mesh.shape["shard"]),
        mesh=mesh,
        in_specs=in_specs,
        out_specs=out_specs,
        check_vma=False,
    )
```
